32 devices in a mesh: groups: 2 (over x), seq: 8 (over z, y), head: 2 (over core).
Axes of the slice: x: 2, y: 2, z: 4, core: 2. Of those that a mesh axis runs over, the one named last changes fastest.
Arguments:
- query_rows: bfloat16 [2048, 4096], P(('groups', 'seq'), 'head'), parts along dimension 0, may hold values from -160 to 160
- key_rows: bfloat16 [2048, 512], P(('groups', 'seq'), 'head'), parts along dimension 0, may hold values from -6 to 6
- value_rows: bfloat16 [2048, 512], P(('groups', 'seq'), 'head'), parts along dimension 0, may hold values from -6 to 6
- grad_out: bfloat16 [2048, 4096], P(('groups', 'seq'), 'head'), parts along dimension 0, may hold values from -6 to 6
- lengths: int32 [64], P(('groups', 'seq')), parts along dimension 0, may hold values from 1 to 640, as said below
Outputs:
- attended: bfloat16 [2048, 4096], P(('groups', 'seq'), 'head'), parts along dimension 0
- grad_query: bfloat16 [2048, 4096], P(('groups', 'seq'), 'head'), parts along dimension 0
- grad_key: bfloat16 [2048, 512], P(('groups', 'seq'), 'head'), parts along dimension 0
- grad_value: bfloat16 [2048, 512], P(('groups', 'seq'), 'head'), parts along dimension 0
The draws below stay inside these ranges and needn't reach their ends.
There are 2 independent parts, one for each index of `groups`. The reference program is written for one: setup_inputs(seed, part) draws one part's arguments, and reference() takes and returns one part's arrays. A program takes and returns all parts, laid end to end along the dimension named above; each array names one. Nothing has to cross between parts.
Inputs may be any that keep to these rules, and one draw needn't show every extreme that they name: The 32 lengths sum to 1024; the first document is the longest, with exactly 640 tokens.
All inputs are finite; a program needn't handle non-finite values.
Results may differ from the reference program's by a relative error of at most 0.035.
Values may be sent and summed in bfloat16 or wider, within the bound.
A program may use at most 64 MiB of HBM per device.

```python
import math
import jax
import jax.numpy as jnp
from jax import lax

HD = 128
QH = 32
KVH = 4
TOKENS = 1024
MOST = 640
NDOC = 32


def shaped_keys(key):
    base = jnp.clip(jax.random.normal(jax.random.fold_in(key, 5), (TOKENS, KVH, HD), jnp.float32), -6.0, 6.0)
    return base


def draw_key_rows(key, part):
    return shaped_keys(key).reshape(TOKENS, KVH * HD).astype(jnp.bfloat16)


def draw_query_rows(key, part):
    group = QH // KVH
    noise = jnp.clip(jax.random.normal(jax.random.fold_in(key, 3), (TOKENS, KVH, group, HD), jnp.float32), -6.0, 6.0)
    rows = noise
    return rows.reshape(TOKENS, QH * HD).astype(jnp.bfloat16)


def draw_lengths(key, part):
    remain = TOKENS - MOST
    others = NDOC - 1
    order = jax.random.permutation(jax.random.fold_in(key, 11), remain - 1)
    cuts = jnp.sort(order[:others - 1].astype(jnp.int32) + 1)
    edges = jnp.concatenate([jnp.zeros((1,), jnp.int32), cuts, jnp.full((1,), remain, jnp.int32)])
    rest = (edges[1:] - edges[:-1]).astype(jnp.int32)
    return jnp.concatenate([jnp.full((1,), MOST, jnp.int32), rest]).astype(jnp.int32)


def block_levels(own_key, shape, cuts, smallest, top_value):
    gain, own = 1.0, jax.random.fold_in(own_key, 6)
    for dim, parts in cuts:
        heights = jnp.exp(jax.random.uniform(jax.random.fold_in(own, dim), (parts,), jnp.float32, smallest / len(cuts), top_value / len(cuts)))
        gain = gain * jnp.repeat(heights, shape[dim] // parts).reshape([-1 if axis == dim else 1 for axis in range(len(shape))])
    return gain


def gaussian(key, shape, deviation, reach, cuts=(), kind=jnp.bfloat16):
    level = block_levels(key, shape, cuts, -0.22, 0.18) if cuts else 1.0
    values = jax.random.normal(key, shape, jnp.float32) * deviation * level
    return jnp.minimum(jnp.maximum(values, -reach), reach).astype(kind)


def setup_inputs(seed: int = 0, part: int = 0) -> dict:
    keys = jax.random.split(jax.random.key(seed), 6)
    part_keys = jax.random.split(jax.random.fold_in(keys[5], part), 6)
    return {
        "query_rows": draw_query_rows(jax.random.fold_in(jax.random.fold_in(keys[5], part), 71), part),
        "key_rows": draw_key_rows(jax.random.fold_in(jax.random.fold_in(keys[5], part), 71), part),
        "value_rows": gaussian(part_keys[2], (TOKENS, KVH * HD), 1.0, 6.0, ((0, 8), (1, 2))),
        "grad_out": gaussian(part_keys[3], (TOKENS, QH * HD), 1.0, 6.0, ((0, 8), (1, 2))),
        "lengths": draw_lengths(jax.random.fold_in(jax.random.fold_in(keys[5], part), 71), part),
    }


def doc_index(ends, positions):
    return lax.optimization_barrier(jnp.sum((ends[None, :] <= positions[:, None]).astype(jnp.int32), axis=1))

def reference(query_rows, key_rows, value_rows, grad_out, lengths):
    group = QH // KVH
    scale = 1.0 / math.sqrt(HD)
    block = math.gcd(TOKENS, 512)
    window = min(TOKENS, MOST + block)
    count = TOKENS // block
    ends = jnp.cumsum(lengths).astype(jnp.int32)
    queries = query_rows.reshape(TOKENS, KVH, group, HD).astype(jnp.float32)
    keyset = key_rows.reshape(TOKENS, KVH, HD).astype(jnp.float32)
    valueset = value_rows.reshape(TOKENS, KVH, HD).astype(jnp.float32)
    cotangent = grad_out.reshape(TOKENS, KVH, group, HD).astype(jnp.float32)

    def one_block(carry, number):
        key_grad, value_grad = carry
        first = number * block
        key_first = jnp.maximum(first + block - window, 0).astype(jnp.int32)
        query_pos = first + jnp.arange(block, dtype=jnp.int32)
        key_pos = key_first + jnp.arange(window, dtype=jnp.int32)
        allowed = (doc_index(ends, query_pos)[:, None] == doc_index(ends, key_pos)[None, :]) & (key_pos[None, :] <= query_pos[:, None])
        allowed = allowed[:, None, None, :]
        query_block = lax.dynamic_slice_in_dim(queries, first, block, 0)
        grad_block = lax.dynamic_slice_in_dim(cotangent, first, block, 0)
        key_block = lax.dynamic_slice_in_dim(keyset, key_first, window, 0)
        value_block = lax.dynamic_slice_in_dim(valueset, key_first, window, 0)
        scores = scale * jnp.einsum('tagd,kad->tagk', query_block, key_block)
        masked = jnp.where(allowed, scores, -1e+30)
        rowmax = lax.optimization_barrier(jnp.max(masked, axis=-1, keepdims=True))
        expo = jnp.where(allowed, jnp.exp(masked - rowmax), 0.0)
        rowsum = lax.optimization_barrier(jnp.sum(expo, axis=-1, keepdims=True))
        weights = lax.optimization_barrier(expo.astype(jnp.bfloat16)).astype(jnp.float32)
        attended = (jnp.einsum('tagk,kad->tagd', weights, value_block) / rowsum).astype(jnp.bfloat16)
        attended_wide = lax.optimization_barrier(attended).astype(jnp.float32)
        lse = rowmax + jnp.log(rowsum)
        delta = lax.optimization_barrier(jnp.sum(grad_block * attended_wide, axis=-1, keepdims=True))
        prob = jnp.where(allowed, jnp.exp(masked - lse), 0.0)
        prob_low = lax.optimization_barrier(prob.astype(jnp.bfloat16)).astype(jnp.float32)
        value_part = jnp.einsum('tagk,tagd->kad', prob_low, grad_block)
        dprob = jnp.einsum('tagd,kad->tagk', grad_block, value_block)
        dscore = lax.optimization_barrier((prob * (dprob - delta)).astype(jnp.bfloat16)).astype(jnp.float32)
        query_grad = (scale * jnp.einsum('tagk,kad->tagd', dscore, key_block)).astype(jnp.bfloat16)
        key_part = jnp.einsum('tagk,tagd->kad', dscore, query_block)
        old_key = lax.dynamic_slice_in_dim(key_grad, key_first, window, 0)
        old_value = lax.dynamic_slice_in_dim(value_grad, key_first, window, 0)
        key_grad = lax.dynamic_update_slice_in_dim(key_grad, old_key + key_part, key_first, 0)
        value_grad = lax.dynamic_update_slice_in_dim(value_grad, old_value + value_part, key_first, 0)
        return ((key_grad, value_grad), (attended, query_grad))
    start = (jnp.zeros((TOKENS, KVH, HD), jnp.float32), jnp.zeros((TOKENS, KVH, HD), jnp.float32))
    (key_grad, value_grad), (attended, query_grad) = lax.scan(one_block, start, jnp.arange(count, dtype=jnp.int32))
    attended = attended.reshape(TOKENS, QH * HD)
    query_grad = query_grad.reshape(TOKENS, QH * HD)
    key_out = (scale * key_grad).astype(jnp.bfloat16).reshape(TOKENS, KVH * HD)
    value_out = value_grad.astype(jnp.bfloat16).reshape(TOKENS, KVH * HD)
    return (attended, query_grad, key_out, value_out)
```

```python
import functools
import math

import jax
import jax.numpy as jnp
from jax import lax
from jax.experimental import pallas as pl
from jax.experimental.pallas import tpu as pltpu
from jax.sharding import PartitionSpec as P

HD = 128
NEGATIVE = -1e30
MESH = pl.DeviceIdType.MESH


def dot_nt(a, b):
    return lax.dot_general(a, b, (((1,), (1,)), ((), ())), preferred_element_type=jnp.float32)


def dot_nn(a, b):
    return lax.dot_general(a, b, (((1,), (0,)), ((), ())), preferred_element_type=jnp.float32)


def kernel(
    devices,
    q_hbm,
    k_hbm,
    v_hbm,
    g_hbm,
    len_ref,
    att_hbm,
    gq_hbm,
    gk_ref,
    gv_ref,
    qs,
    gs,
    kbuf,
    vbuf,
    sbuf,
    dbuf,
    oacc,
    qacc,
    ostage,
    qstage,
    gsend,
    grecv,
    gown,
    lens,
    start_ref,
    rowmax,
    rowsum,
    delta,
    load_sem,
    kv_sem,
    store_sem,
    k_send,
    k_recv,
    v_send,
    v_recv,
    g_send,
    g_recv,
    l_send,
    l_recv,
):
    heads, rows, _ = qs.shape
    tok = kbuf.shape[1]
    group = rows // tok
    docs = len_ref.shape[0]
    reach = kbuf.shape[0]
    scale = 1.0 / math.sqrt(HD)
    to_exp2 = scale * math.log2(math.e)

    idx = lax.axis_index("seq")
    in_first = idx < reach
    base = jnp.where(in_first, 0, reach)
    local = idx - base
    after = jnp.where(in_first, reach, devices) - base

    own_k = pltpu.make_async_copy(k_hbm, kbuf.at[local], kv_sem.at[0])
    own_v = pltpu.make_async_copy(v_hbm, vbuf.at[local], kv_sem.at[1])
    own_k.start()
    own_v.start()
    loads = []
    for n, (source, target) in enumerate(((q_hbm, qs), (g_hbm, gs))):
        for a in range(heads):
            for h in range(group):
                column = (a * group + h) * HD
                loads.append(
                    pltpu.make_async_copy(
                        source.at[:, pl.ds(column, HD)],
                        target.at[a, pl.ds(h * tok, tok), :],
                        load_sem.at[n, a, h],
                    )
                )
    for copy in loads:
        copy.start()

    barrier = pltpu.get_barrier_semaphore()

    def greet(step, _):
        other = lax.rem(idx + step, devices)
        pl.semaphore_signal(barrier, inc=1, device_id={"seq": other}, device_id_type=MESH)
        return 0

    lax.fori_loop(1, devices, greet, 0)

    lens[idx] = jnp.zeros(lens.shape[1:], jnp.int32)
    for n in range(docs):
        lens[idx, n : n + 1, :] = jnp.full((1, HD), len_ref[n], jnp.int32)
    rowmax[...] = jnp.full(rowmax.shape, NEGATIVE, jnp.float32)
    rowsum[...] = jnp.zeros(rowsum.shape, jnp.float32)
    delta[...] = jnp.zeros(delta.shape, jnp.float32)
    start_ref[...] = jnp.zeros(start_ref.shape, jnp.int32)
    own_k.wait()
    own_v.wait()
    pl.semaphore_wait(barrier, devices - 1)

    def k_copy(target):
        return pltpu.make_async_remote_copy(
            src_ref=kbuf.at[local],
            dst_ref=kbuf.at[local],
            send_sem=k_send.at[target],
            recv_sem=k_recv.at[local],
            device_id={"seq": base + target},
            device_id_type=MESH,
        )

    def v_copy(target):
        return pltpu.make_async_remote_copy(
            src_ref=vbuf.at[local],
            dst_ref=vbuf.at[local],
            send_sem=v_send.at[target],
            recv_sem=v_recv.at[local],
            device_id={"seq": base + target},
            device_id_type=MESH,
        )

    def l_copy(target):
        return pltpu.make_async_remote_copy(
            src_ref=lens.at[idx],
            dst_ref=lens.at[idx],
            send_sem=l_send.at[target],
            recv_sem=l_recv.at[idx],
            device_id={"seq": target},
            device_id_type=MESH,
        )

    def arrival(buf, sem, slot):
        return pltpu.make_async_remote_copy(
            src_ref=buf.at[slot],
            dst_ref=buf.at[slot],
            send_sem=sem.at[slot],
            recv_sem=sem.at[slot],
            device_id={"seq": idx},
            device_id_type=MESH,
        )

    def start_k(n, _):
        k_copy(after - 1 - n).start()
        return 0

    def start_v(n, _):
        v_copy(after - 1 - n).start()
        return 0

    def start_l(target, _):
        @pl.when(target != idx)
        def _():
            l_copy(target).start()

        return 0

    lax.fori_loop(0, after - 1 - local, start_k, 0)
    lax.fori_loop(reach, devices, start_l, 0)
    lax.fori_loop(0, after - 1 - local, start_v, 0)

    for copy in loads[: heads * group]:
        copy.wait()

    @pl.when(jnp.logical_not(in_first))
    def _():
        position = idx * tok + lax.broadcasted_iota(jnp.int32, (1, tok), 1)

        def one(source, carry):
            @pl.when(source != idx)
            def _():
                arrival(lens, l_recv, source).wait_recv()

            total, first = carry
            for n in range(docs):
                total = total + lens[source, n : n + 1, :]
                first = jnp.where(total <= position, total, first)
            return total, first

        zero = jnp.zeros((1, tok), jnp.int32)
        _, first = lax.fori_loop(0, devices, one, (zero, zero))
        start_ref[0:1, :] = first

    key_index = lax.broadcasted_iota(jnp.int32, (tok, tok), 0)
    query_index = lax.broadcasted_iota(jnp.int32, (tok, tok), 1)

    def scores(j, diagonal):
        allowed = (base + j) * tok + key_index >= start_ref[0:1, :]
        if diagonal:
            allowed = allowed & (key_index <= query_index)
        for a in range(heads):
            keys = kbuf[j, :, a * HD : (a + 1) * HD]
            raw = dot_nt(keys, qs[a])
            for h in range(group):
                cols = slice(h * tok, (h + 1) * tok)
                masked = jnp.where(allowed, raw[:, cols], NEGATIVE)
                sbuf[j, a, :, cols] = masked
                rowmax[a, :, cols] = jnp.maximum(
                    rowmax[a, :, cols], jnp.max(masked, axis=0, keepdims=True)
                )

    scores(local, True)

    def scores_step(n, _):
        j = local - 1 - n
        arrival(kbuf, k_recv, j).wait_recv()
        scores(j, False)
        return 0

    lax.fori_loop(0, local, scores_step, 0)

    for copy in loads[heads * group :]:
        copy.wait()

    def weights(j):
        for a in range(heads):
            values = vbuf[j, :, a * HD : (a + 1) * HD]
            dprob = dot_nt(values, gs[a])
            for h in range(group):
                cols = slice(h * tok, (h + 1) * tok)
                expo = jnp.exp2((sbuf[j, a, :, cols] - rowmax[a, :, cols]) * to_exp2)
                sbuf[j, a, :, cols] = expo
                part = dprob[:, cols]
                dbuf[j, a, :, cols] = part
                rowsum[a, :, cols] += jnp.sum(expo, axis=0, keepdims=True)
                delta[a, :, cols] += jnp.sum(expo * part, axis=0, keepdims=True)

    weights(local)

    def weights_step(n, _):
        j = local - 1 - n
        arrival(vbuf, v_recv, j).wait_recv()
        weights(j)
        return 0

    lax.fori_loop(0, local, weights_step, 0)

    rowsum[...] = 1.0 / rowsum[...]
    delta[...] = delta[...] * rowsum[...]
    oacc[...] = jnp.zeros(oacc.shape, jnp.float32)
    qacc[...] = jnp.zeros(qacc.shape, jnp.float32)

    def gradients(j, store):
        for a in range(heads):
            prob = sbuf[j, a] * rowsum[a]
            prob_low = prob.astype(jnp.bfloat16)
            dscore = (prob * (dbuf[j, a] - delta[a])).astype(jnp.bfloat16)
            cols = slice(a * HD, (a + 1) * HD)
            store(cols, dot_nn(dscore, qs[a]), dot_nn(prob_low, gs[a]))
            oacc[a] += dot_nn(vbuf[j, :, cols].T, prob_low)
            qacc[a] += dot_nn(kbuf[j, :, cols].T, dscore)

    def g_copy(j):
        return pltpu.make_async_remote_copy(
            src_ref=gsend.at[j],
            dst_ref=grecv.at[local],
            send_sem=g_send.at[j],
            recv_sem=g_recv.at[local],
            device_id={"seq": base + j},
            device_id_type=MESH,
        )

    def gradients_step(j, _):
        def store(cols, key_part, value_part):
            gsend[j, 0, :, cols] = key_part.astype(jnp.bfloat16)
            gsend[j, 1, :, cols] = value_part.astype(jnp.bfloat16)

        gradients(j, store)
        g_copy(j).start()
        return 0

    lax.fori_loop(0, local, gradients_step, 0)

    def store_own(cols, key_part, value_part):
        gown[0, :, cols] = key_part
        gown[1, :, cols] = value_part

    gradients(local, store_own)

    stores = []
    for a in range(heads):
        for h in range(group):
            cols = slice(h * tok, (h + 1) * tok)
            ostage[a, cols, :] = oacc[a, :, cols].T.astype(jnp.bfloat16)
            qstage[a, cols, :] = (scale * qacc[a, :, cols]).T.astype(jnp.bfloat16)
            column = (a * group + h) * HD
            for n, (source, target) in enumerate(((ostage, att_hbm), (qstage, gq_hbm))):
                copy = pltpu.make_async_copy(
                    source.at[a, pl.ds(h * tok, tok), :],
                    target.at[:, pl.ds(column, HD)],
                    store_sem.at[n, a, h],
                )
                copy.start()
                stores.append(copy)

    def collect(j, _):
        arrival(grecv, g_recv, j).wait_recv()
        gown[...] += grecv[j].astype(jnp.float32)
        return 0

    lax.fori_loop(local + 1, after, collect, 0)
    gk_ref[...] = (scale * gown[0]).astype(jnp.bfloat16)
    gv_ref[...] = gown[1].astype(jnp.bfloat16)

    for copy in stores:
        copy.wait()

    def end_kv(target, _):
        k_copy(target).wait_send()
        v_copy(target).wait_send()
        return 0

    def end_l(target, _):
        @pl.when(target != idx)
        def _():
            l_copy(target).wait_send()

        return 0

    def end_g(j, _):
        g_copy(j).wait_send()
        return 0

    lax.fori_loop(local + 1, after, end_kv, 0)
    lax.fori_loop(reach, devices, end_l, 0)
    lax.fori_loop(0, local, end_g, 0)


def shards(query_rows, key_rows, value_rows, grad_out, lengths):
    tok, width = query_rows.shape
    heads = key_rows.shape[1] // HD
    group = width // HD // heads
    devices = lax.axis_size("seq")
    reach = devices // 2 + 1
    rows = group * tok
    docs = -(-lengths.shape[0] // 8) * 8
    anywhere = pl.BlockSpec(memory_space=pl.ANY)
    vmem = pl.BlockSpec(memory_space=pltpu.VMEM)
    dma = pltpu.SemaphoreType.DMA
    bf16, f32 = jnp.bfloat16, jnp.float32
    pairs = devices * rows * tok * heads
    return pl.pallas_call(
        functools.partial(kernel, devices),
        out_shape=(
            jax.ShapeDtypeStruct(query_rows.shape, bf16),
            jax.ShapeDtypeStruct(query_rows.shape, bf16),
            jax.ShapeDtypeStruct(key_rows.shape, bf16),
            jax.ShapeDtypeStruct(value_rows.shape, bf16),
        ),
        in_specs=[anywhere] * 4 + [pl.BlockSpec(memory_space=pltpu.SMEM)],
        out_specs=(anywhere, anywhere, vmem, vmem),
        scratch_shapes=[
            pltpu.VMEM((heads, rows, HD), bf16),
            pltpu.VMEM((heads, rows, HD), bf16),
            pltpu.VMEM((reach, tok, heads * HD), bf16),
            pltpu.VMEM((reach, tok, heads * HD), bf16),
            pltpu.VMEM((reach, heads, tok, rows), f32),
            pltpu.VMEM((reach, heads, tok, rows), f32),
            pltpu.VMEM((heads, HD, rows), f32),
            pltpu.VMEM((heads, HD, rows), f32),
            pltpu.VMEM((heads, rows, HD), bf16),
            pltpu.VMEM((heads, rows, HD), bf16),
            pltpu.VMEM((reach, 2, tok, heads * HD), bf16),
            pltpu.VMEM((reach, 2, tok, heads * HD), bf16),
            pltpu.VMEM((2, tok, heads * HD), f32),
            pltpu.VMEM((devices, docs, HD), jnp.int32),
            pltpu.VMEM((8, tok), jnp.int32),
            pltpu.VMEM((heads, 1, rows), f32),
            pltpu.VMEM((heads, 1, rows), f32),
            pltpu.VMEM((heads, 1, rows), f32),
            dma((2, heads, group)),
            dma((2,)),
            dma((2, heads, group)),
            dma((reach,)),
            dma((reach,)),
            dma((reach,)),
            dma((reach,)),
            dma((reach,)),
            dma((reach,)),
            dma((devices,)),
            dma((devices,)),
        ],
        compiler_params=pltpu.CompilerParams(
            collective_id=0, has_side_effects=True, vmem_limit_bytes=56 * 1024 * 1024
        ),
        cost_estimate=pl.CostEstimate(
            flops=6 * pairs * HD, bytes_accessed=8 * tok * width, transcendentals=pairs
        ),
    )(query_rows, key_rows, value_rows, grad_out, lengths)


def solution(mesh):
    split = P(("groups", "seq"), "head")
    return jax.shard_map(
        shards,
        mesh=mesh,
        in_specs=(split, split, split, split, P(("groups", "seq"))),
        out_specs=(split, split, split, split),
        check_vma=False,
    )
```

```python
import functools
import math

import jax
import jax.numpy as jnp
from jax import lax
from jax.experimental import pallas as pl
from jax.experimental.pallas import tpu as pltpu
from jax.sharding import PartitionSpec as P

HD = 128
NEGATIVE = -1e30
MESH = pl.DeviceIdType.MESH
UNROLLED = 8


def dot_nt(a, b):
    return lax.dot_general(a, b, (((1,), (1,)), ((), ())), preferred_element_type=jnp.float32)


def dot_nn(a, b):
    return lax.dot_general(a, b, (((1,), (0,)), ((), ())), preferred_element_type=jnp.float32)


def stacked(ref, first, count):
    return jnp.concatenate(
        [ref[:, (first + h) * HD : (first + h + 1) * HD] for h in range(count)], axis=0
    )


def kernel(
    devices,
    q_hbm,
    k_hbm,
    v_hbm,
    g_hbm,
    len_ref,
    att_hbm,
    gq_hbm,
    gk_ref,
    gv_ref,
    qbuf,
    gbuf,
    kv,
    probs,
    dscores,
    ostage,
    qstage,
    gsend,
    grecv,
    gown,
    lens,
    start_ref,
    load_sem,
    kv_sem,
    store_sem,
    kv_send,
    kv_recv,
    g_send,
    g_recv,
    l_send,
    l_recv,
    *loop_refs,
):
    heads, reach, _, tok, _ = kv.shape
    group = qbuf.shape[1] // HD // heads
    docs = len_ref.shape[0]
    scale = 1.0 / math.sqrt(HD)
    to_exp2 = scale * math.log2(math.e)
    wide = 2 if group % 2 == 0 else 1

    idx = lax.axis_index("seq")
    in_first = idx < reach
    base = jnp.where(in_first, 0, reach)
    local = idx - base
    after = jnp.where(in_first, reach, devices) - base

    own = []
    for a in range(heads):
        for n, source in enumerate((k_hbm, v_hbm)):
            own.append(
                pltpu.make_async_copy(
                    source.at[:, pl.ds(a * HD, HD)], kv.at[a, local, n], kv_sem.at[a, n]
                )
            )
    loads = []
    for a in range(heads):
        cols = pl.ds(a * group * HD, group * HD)
        for n, (source, target) in enumerate(((q_hbm, qbuf), (g_hbm, gbuf))):
            loads.append(
                pltpu.make_async_copy(source.at[:, cols], target.at[:, cols], load_sem.at[a, n])
            )
    for copy in own + loads:
        copy.start()

    barrier = pltpu.get_barrier_semaphore()

    def greet(step, _):
        other = lax.rem(idx + step, devices)
        pl.semaphore_signal(barrier, inc=1, device_id={"seq": other}, device_id_type=MESH)
        return 0

    lax.fori_loop(1, devices, greet, 0)

    lens[idx] = jnp.zeros(lens.shape[1:], jnp.int32)
    for n in range(docs):
        lens[idx, n : n + 1, :] = jnp.full((1, HD), len_ref[n], jnp.int32)
    start_ref[...] = jnp.zeros(start_ref.shape, jnp.int32)
    for copy in own:
        copy.wait()
    pl.semaphore_wait(barrier, devices - 1)

    def l_copy(target):
        return pltpu.make_async_remote_copy(
            src_ref=lens.at[idx],
            dst_ref=lens.at[idx],
            send_sem=l_send.at[target],
            recv_sem=l_recv.at[idx],
            device_id={"seq": target},
            device_id_type=MESH,
        )

    def kv_copy(a, target):
        return pltpu.make_async_remote_copy(
            src_ref=kv.at[a, local],
            dst_ref=kv.at[a, local],
            send_sem=kv_send.at[a, target],
            recv_sem=kv_recv.at[a, local],
            device_id={"seq": base + target},
            device_id_type=MESH,
        )

    def g_copy(a, j):
        return pltpu.make_async_remote_copy(
            src_ref=gsend.at[a, j],
            dst_ref=grecv.at[a, local],
            send_sem=g_send.at[a, j],
            recv_sem=g_recv.at[a, local],
            device_id={"seq": base + j},
            device_id_type=MESH,
        )

    def arrival(buf, sem):
        return pltpu.make_async_remote_copy(
            src_ref=buf,
            dst_ref=buf,
            send_sem=sem,
            recv_sem=sem,
            device_id={"seq": idx},
            device_id_type=MESH,
        )

    def start_l(target, _):
        @pl.when(target != idx)
        def _():
            l_copy(target).start()

        return 0

    lax.fori_loop(reach, devices, start_l, 0)
    for a in range(heads):

        def start_kv(n, _, a=a):
            kv_copy(a, after - 1 - n).start()
            return 0

        lax.fori_loop(0, after - 1 - local, start_kv, 0)

    @pl.when(jnp.logical_not(in_first))
    def _():
        position = idx * tok + lax.broadcasted_iota(jnp.int32, (1, tok), 1)

        def one(source, carry):
            @pl.when(source != idx)
            def _():
                arrival(lens.at[source], l_recv.at[source]).wait_recv()

            total, first = carry
            for n in range(docs):
                total = total + lens[source, n : n + 1, :]
                first = jnp.where(total <= position, total, first)
            return total, first

        zero = jnp.zeros((1, tok), jnp.int32)
        _, first = lax.fori_loop(0, devices, one, (zero, zero))
        for h in range(wide):
            start_ref[0:1, h * tok : (h + 1) * tok] = first

    def one_count(count):
        size = count * tok
        key_index = lax.broadcasted_iota(jnp.int32, (size, wide * tok), 0)
        query_index = lax.rem(lax.broadcasted_iota(jnp.int32, (tok, wide * tok), 1), tok)
        causal = lax.broadcasted_iota(jnp.int32, (tok, wide * tok), 0) <= query_index
        for a in range(heads):
            for j in range(count - 1):
                arrival(kv.at[a, j], kv_recv.at[a, j]).wait_recv()
            loads[2 * a].wait()
            loads[2 * a + 1].wait()
            keys = kv[a, 0:count, 0].reshape(size, HD)
            values = kv[a, 0:count, 1].reshape(size, HD)
            keys_t = keys.T
            values_t = values.T
            for p in range(group // wide):
                first = a * group + p * wide
                queries = stacked(qbuf, first, wide)
                cotangents = stacked(gbuf, first, wide)
                raw = dot_nt(keys, queries)
                if count <= devices - reach:
                    raw = jnp.where(base * tok + key_index >= start_ref[0:1, :], raw, NEGATIVE)
                last = jnp.where(causal, raw[size - tok :], NEGATIVE)
                raw = jnp.concatenate([raw[: size - tok], last], axis=0) if count > 1 else last
                rowmax = jnp.max(raw, axis=0, keepdims=True)
                expo = jnp.exp2((raw - rowmax) * to_exp2)
                dprob = dot_nt(values, cotangents)
                inverse = 1.0 / jnp.sum(expo, axis=0, keepdims=True)
                delta = jnp.sum(expo * dprob, axis=0, keepdims=True) * inverse
                prob = expo * inverse
                prob_low = prob.astype(jnp.bfloat16)
                dscore = (prob * (dprob - delta)).astype(jnp.bfloat16)
                wide_cols = slice(p * wide * tok, (p + 1) * wide * tok)
                probs[0:size, wide_cols] = prob_low
                dscores[0:size, wide_cols] = dscore
                out = dot_nn(values_t, prob_low)
                grad = scale * dot_nn(keys_t, dscore)
                for h in range(wide):
                    cols = slice((first + h) * HD, (first + h + 1) * HD)
                    part = slice(h * tok, (h + 1) * tok)
                    ostage[:, cols] = out[:, part].T.astype(jnp.bfloat16)
                    qstage[:, cols] = grad[:, part].T.astype(jnp.bfloat16)
            key_part = dot_nn(dscores[0:size, :], stacked(qbuf, a * group, group))
            value_part = dot_nn(probs[0:size, :], stacked(gbuf, a * group, group))
            for j in range(count - 1):
                piece = slice(j * tok, (j + 1) * tok)
                gsend[a, j, 0] = key_part[piece].astype(jnp.bfloat16)
                gsend[a, j, 1] = value_part[piece].astype(jnp.bfloat16)
                g_copy(a, j).start()
            gown[a, 0] = key_part[size - tok :]
            gown[a, 1] = value_part[size - tok :]

    def any_count(sbuf, dbuf, oacc, qacc, rowmax, rowsum, delta):
        key_index = lax.broadcasted_iota(jnp.int32, (tok, tok), 0)
        query_index = lax.broadcasted_iota(jnp.int32, (tok, tok), 1)
        for a in range(heads):
            loads[2 * a].wait()
            loads[2 * a + 1].wait()
            queries = stacked(qbuf, a * group, group)
            cotangents = stacked(gbuf, a * group, group)
            rowmax[...] = jnp.full(rowmax.shape, NEGATIVE, jnp.float32)
            rowsum[...] = jnp.zeros(rowsum.shape, jnp.float32)
            delta[...] = jnp.zeros(delta.shape, jnp.float32)
            oacc[...] = jnp.zeros(oacc.shape, jnp.float32)
            qacc[...] = jnp.zeros(qacc.shape, jnp.float32)

            def first_pass(j, diagonal):
                allowed = (base + j) * tok + key_index >= start_ref[0:1, 0:tok]
                if diagonal:
                    allowed = allowed & (key_index <= query_index)
                raw = dot_nt(kv[a, j, 0], queries)
                for h in range(group):
                    cols = slice(h * tok, (h + 1) * tok)
                    masked = jnp.where(allowed, raw[:, cols], NEGATIVE)
                    sbuf[j, :, cols] = masked
                    rowmax[:, cols] = jnp.maximum(
                        rowmax[:, cols], jnp.max(masked, axis=0, keepdims=True)
                    )

            def first_step(j, _):
                arrival(kv.at[a, j], kv_recv.at[a, j]).wait_recv()
                first_pass(j, False)
                return 0

            first_pass(local, True)
            lax.fori_loop(0, local, first_step, 0)

            def second_step(j, _):
                dprob = dot_nt(kv[a, j, 1], cotangents)
                expo = jnp.exp2((sbuf[j] - rowmax[...]) * to_exp2)
                sbuf[j] = expo
                dbuf[j] = dprob
                rowsum[...] += jnp.sum(expo, axis=0, keepdims=True)
                delta[...] += jnp.sum(expo * dprob, axis=0, keepdims=True)
                return 0

            lax.fori_loop(0, local + 1, second_step, 0)
            rowsum[...] = 1.0 / rowsum[...]
            delta[...] = delta[...] * rowsum[...]

            def third_pass(j):
                prob = sbuf[j] * rowsum[...]
                prob_low = prob.astype(jnp.bfloat16)
                dscore = (prob * (dbuf[j] - delta[...])).astype(jnp.bfloat16)
                oacc[...] += dot_nn(kv[a, j, 1].T, prob_low)
                qacc[...] += dot_nn(kv[a, j, 0].T, dscore)
                return dot_nn(dscore, queries), dot_nn(prob_low, cotangents)

            def third_step(j, _):
                key_part, value_part = third_pass(j)
                gsend[a, j, 0] = key_part.astype(jnp.bfloat16)
                gsend[a, j, 1] = value_part.astype(jnp.bfloat16)
                g_copy(a, j).start()
                return 0

            lax.fori_loop(0, local, third_step, 0)
            gown[a, 0], gown[a, 1] = third_pass(local)
            for h in range(group):
                cols = slice((a * group + h) * HD, (a * group + h + 1) * HD)
                part = slice(h * tok, (h + 1) * tok)
                ostage[:, cols] = oacc[:, part].T.astype(jnp.bfloat16)
                qstage[:, cols] = (scale * qacc[:, part]).T.astype(jnp.bfloat16)

    if loop_refs:
        any_count(*loop_refs)
    else:
        for count in range(1, reach + 1):
            pl.when(local + 1 == count)(functools.partial(one_count, count))

    stores = [
        pltpu.make_async_copy(ostage, att_hbm, store_sem.at[0]),
        pltpu.make_async_copy(qstage, gq_hbm, store_sem.at[1]),
    ]
    for copy in stores:
        copy.start()

    for a in range(heads):

        def collect(j, _, a=a):
            arrival(grecv.at[a, j], g_recv.at[a, j]).wait_recv()
            gown[a] += grecv[a, j].astype(jnp.float32)
            return 0

        lax.fori_loop(local + 1, after, collect, 0)
        cols = slice(a * HD, (a + 1) * HD)
        gk_ref[:, cols] = (scale * gown[a, 0]).astype(jnp.bfloat16)
        gv_ref[:, cols] = gown[a, 1].astype(jnp.bfloat16)

    for copy in stores:
        copy.wait()

    def end_l(target, _):
        @pl.when(target != idx)
        def _():
            l_copy(target).wait_send()

        return 0

    lax.fori_loop(reach, devices, end_l, 0)
    for a in range(heads):

        def end_kv(target, _, a=a):
            kv_copy(a, target).wait_send()
            return 0

        def end_g(j, _, a=a):
            g_copy(a, j).wait_send()
            return 0

        lax.fori_loop(local + 1, after, end_kv, 0)
        lax.fori_loop(0, local, end_g, 0)


def hand_on(*refs):
    count = len(refs) // 2
    sems = refs[-1]
    copies = [
        pltpu.make_async_copy(refs[n], refs[count + n], sems.at[n]) for n in range(count)
    ]
    for copy in copies:
        copy.start()
    for copy in copies:
        copy.wait()


def shards(query_rows, key_rows, value_rows, grad_out, lengths):
    tok, width = query_rows.shape
    heads = key_rows.shape[1] // HD
    group = width // HD // heads
    devices = lax.axis_size("seq")
    reach = devices // 2 + 1
    rows = group * tok
    docs = -(-lengths.shape[0] // 8) * 8
    wide = 2 if group % 2 == 0 else 1
    unrolled = reach <= UNROLLED
    held = reach * tok if unrolled else 16
    anywhere = pl.BlockSpec(memory_space=pl.ANY)
    vmem = pl.BlockSpec(memory_space=pltpu.VMEM)
    dma = pltpu.SemaphoreType.DMA
    bf16, f32 = jnp.bfloat16, jnp.float32
    loop_scratch = [
        pltpu.VMEM((reach, tok, rows), f32),
        pltpu.VMEM((reach, tok, rows), f32),
        pltpu.VMEM((HD, rows), f32),
        pltpu.VMEM((HD, rows), f32),
        pltpu.VMEM((1, rows), f32),
        pltpu.VMEM((1, rows), f32),
        pltpu.VMEM((1, rows), f32),
    ]
    pairs = reach * rows * tok * heads
    shapes = (
        jax.ShapeDtypeStruct(query_rows.shape, bf16),
        jax.ShapeDtypeStruct(query_rows.shape, bf16),
        jax.ShapeDtypeStruct(key_rows.shape, bf16),
        jax.ShapeDtypeStruct(value_rows.shape, bf16),
    )
    results = pl.pallas_call(
        functools.partial(kernel, devices),
        out_shape=shapes,
        in_specs=[anywhere] * 4 + [pl.BlockSpec(memory_space=pltpu.SMEM)],
        out_specs=(anywhere, anywhere, vmem, vmem),
        scratch_shapes=[
            pltpu.VMEM((tok, width), bf16),
            pltpu.VMEM((tok, width), bf16),
            pltpu.VMEM((heads, reach, 2, tok, HD), bf16),
            pltpu.VMEM((held, rows), bf16),
            pltpu.VMEM((held, rows), bf16),
            pltpu.VMEM((tok, width), bf16),
            pltpu.VMEM((tok, width), bf16),
            pltpu.VMEM((heads, reach, 2, tok, HD), bf16),
            pltpu.VMEM((heads, reach, 2, tok, HD), bf16),
            pltpu.VMEM((heads, 2, tok, HD), f32),
            pltpu.VMEM((devices, docs, HD), jnp.int32),
            pltpu.VMEM((1, wide * tok), jnp.int32),
            dma((heads, 2)),
            dma((heads, 2)),
            dma((2,)),
            dma((heads, reach)),
            dma((heads, reach)),
            dma((heads, reach)),
            dma((heads, reach)),
            dma((devices,)),
            dma((devices,)),
        ]
        + ([] if unrolled else loop_scratch),
        compiler_params=pltpu.CompilerParams(
            collective_id=0, has_side_effects=True, vmem_limit_bytes=56 * 1024 * 1024
        ),
        cost_estimate=pl.CostEstimate(
            flops=12 * pairs * HD, bytes_accessed=8 * tok * width, transcendentals=pairs
        ),
    )(query_rows, key_rows, value_rows, grad_out, lengths)
    return pl.pallas_call(
        hand_on,
        out_shape=shapes,
        in_specs=[anywhere] * 4,
        out_specs=(anywhere,) * 4,
        scratch_shapes=[dma((4,))],
        cost_estimate=pl.CostEstimate(
            flops=0, bytes_accessed=8 * tok * width, transcendentals=0
        ),
    )(*results)


def solution(mesh):
    split = P(("groups", "seq"), "head")
    return jax.shard_map(
        shards,
        mesh=mesh,
        in_specs=(split, split, split, split, P(("groups", "seq"))),
        out_specs=(split, split, split, split),
        check_vma=False,
    )
```

```python
import functools
import math

import jax
import jax.numpy as jnp
from jax import lax
from jax.experimental import pallas as pl
from jax.experimental.pallas import tpu as pltpu
from jax.sharding import PartitionSpec as P

HD = 128
NEGATIVE = -1e30
MESH = pl.DeviceIdType.MESH
UNROLLED = 8


def dot_nt(a, b):
    return lax.dot_general(a, b, (((1,), (1,)), ((), ())), preferred_element_type=jnp.float32)


def dot_nn(a, b):
    return lax.dot_general(a, b, (((1,), (0,)), ((), ())), preferred_element_type=jnp.float32)


def stacked(ref, first, count):
    return jnp.concatenate(
        [ref[:, (first + h) * HD : (first + h + 1) * HD] for h in range(count)], axis=0
    )


def kernel(
    devices,
    q_hbm,
    k_hbm,
    v_hbm,
    g_hbm,
    len_ref,
    att_hbm,
    gq_hbm,
    gk_ref,
    gv_ref,
    qbuf,
    gbuf,
    kv,
    probs,
    dscores,
    ostage,
    qstage,
    gsend,
    grecv,
    gown,
    lens,
    start_ref,
    load_sem,
    kv_sem,
    store_sem,
    kv_send,
    kv_recv,
    g_send,
    g_recv,
    l_send,
    l_recv,
    kv_relay,
    g_relay,
    kr_send,
    kr_recv,
    gr_send,
    gr_recv,
    kf_send,
    gf_send,
    *loop_refs,
):
    heads, reach, _, tok, _ = kv.shape
    relaying = not loop_refs and reach < devices
    relayed = [j for j in range(reach - 1) if (reach - 1 - j) % 2] if relaying else []
    group = qbuf.shape[1] // HD // heads
    docs = len_ref.shape[0]
    scale = 1.0 / math.sqrt(HD)
    to_exp2 = scale * math.log2(math.e)
    wide = 2 if group % 2 == 0 else 1

    idx = lax.axis_index("seq")
    in_first = idx < reach
    base = jnp.where(in_first, 0, reach)
    local = idx - base
    after = jnp.where(in_first, reach, devices) - base

    own = []
    for a in range(heads):
        for n, source in enumerate((k_hbm, v_hbm)):
            own.append(
                pltpu.make_async_copy(
                    source.at[:, pl.ds(a * HD, HD)], kv.at[a, local, n], kv_sem.at[a, n]
                )
            )
    loads = []
    for a in range(heads):
        cols = pl.ds(a * group * HD, group * HD)
        for n, (source, target) in enumerate(((q_hbm, qbuf), (g_hbm, gbuf))):
            loads.append(
                pltpu.make_async_copy(source.at[:, cols], target.at[:, cols], load_sem.at[a, n])
            )
    for copy in own + loads:
        copy.start()

    barrier = pltpu.get_barrier_semaphore()

    def greet(step, _):
        other = lax.rem(idx + step, devices)
        pl.semaphore_signal(barrier, inc=1, device_id={"seq": other}, device_id_type=MESH)
        return 0

    lax.fori_loop(1, devices, greet, 0)

    lens[idx] = jnp.zeros(lens.shape[1:], jnp.int32)
    for n in range(docs):
        lens[idx, n : n + 1, :] = jnp.full((1, HD), len_ref[n], jnp.int32)
    start_ref[...] = jnp.zeros(start_ref.shape, jnp.int32)
    for copy in own:
        copy.wait()
    pl.semaphore_wait(barrier, devices - 1)

    def l_copy(target):
        return pltpu.make_async_remote_copy(
            src_ref=lens.at[idx],
            dst_ref=lens.at[idx],
            send_sem=l_send.at[target],
            recv_sem=l_recv.at[idx],
            device_id={"seq": target},
            device_id_type=MESH,
        )

    def kv_copy(a, target):
        return pltpu.make_async_remote_copy(
            src_ref=kv.at[a, local],
            dst_ref=kv.at[a, local],
            send_sem=kv_send.at[a, target],
            recv_sem=kv_recv.at[a, local],
            device_id={"seq": base + target},
            device_id_type=MESH,
        )

    def g_copy(a, j):
        return pltpu.make_async_remote_copy(
            src_ref=gsend.at[a, j],
            dst_ref=grecv.at[a, local],
            send_sem=g_send.at[a, j],
            recv_sem=g_recv.at[a, local],
            device_id={"seq": base + j},
            device_id_type=MESH,
        )

    def kv_to_relay(a, j):
        return pltpu.make_async_remote_copy(
            src_ref=kv.at[a, j],
            dst_ref=kv_relay.at[a, j],
            send_sem=kr_send.at[a],
            recv_sem=kr_recv.at[a, j],
            device_id={"seq": reach},
            device_id_type=MESH,
        )

    def kv_forward(a, j):
        return pltpu.make_async_remote_copy(
            src_ref=kv_relay.at[a, j],
            dst_ref=kv.at[a, j],
            send_sem=kf_send.at[a, j],
            recv_sem=kv_recv.at[a, j],
            device_id={"seq": reach - 1},
            device_id_type=MESH,
        )

    def g_to_relay(a, j):
        return pltpu.make_async_remote_copy(
            src_ref=gsend.at[a, j],
            dst_ref=g_relay.at[a, j],
            send_sem=gr_send.at[a, j],
            recv_sem=gr_recv.at[a, j],
            device_id={"seq": reach},
            device_id_type=MESH,
        )

    def g_forward(a, j):
        return pltpu.make_async_remote_copy(
            src_ref=g_relay.at[a, j],
            dst_ref=grecv.at[a, reach - 1],
            send_sem=gf_send.at[a, j],
            recv_sem=g_recv.at[a, reach - 1],
            device_id={"seq": j},
            device_id_type=MESH,
        )

    def is_relayed(j):
        found = idx < 0
        for other in relayed:
            found = jnp.logical_or(found, j == other)
        return found

    def arrival(buf, sem):
        return pltpu.make_async_remote_copy(
            src_ref=buf,
            dst_ref=buf,
            send_sem=sem,
            recv_sem=sem,
            device_id={"seq": idx},
            device_id_type=MESH,
        )

    def start_l(target, _):
        @pl.when(target != idx)
        def _():
            l_copy(target).start()

        return 0

    skip = jnp.where(in_first & is_relayed(idx), 1, 0)
    lax.fori_loop(reach, devices, start_l, 0)
    for a in range(heads):
        for j in relayed:
            pl.when(idx == j)(kv_to_relay(a, j).start)

        def start_kv(n, _, a=a):
            kv_copy(a, after - 1 - n).start()
            return 0

        lax.fori_loop(skip, after - 1 - local, start_kv, 0)

    if relaying:

        @pl.when(idx == reach)
        def _():
            for a in range(heads):
                for j in relayed:
                    kv_to_relay(a, j).wait_recv()
                    kv_forward(a, j).start()

    @pl.when(jnp.logical_not(in_first))
    def _():
        position = idx * tok + lax.broadcasted_iota(jnp.int32, (1, tok), 1)

        def one(source, carry):
            @pl.when(source != idx)
            def _():
                arrival(lens.at[source], l_recv.at[source]).wait_recv()

            total, first = carry
            for n in range(docs):
                total = total + lens[source, n : n + 1, :]
                first = jnp.where(total <= position, total, first)
            return total, first

        zero = jnp.zeros((1, tok), jnp.int32)
        _, first = lax.fori_loop(0, devices, one, (zero, zero))
        for h in range(wide):
            start_ref[0:1, h * tok : (h + 1) * tok] = first

    def one_count(count):
        size = count * tok
        key_index = lax.broadcasted_iota(jnp.int32, (size, wide * tok), 0)
        query_index = lax.rem(lax.broadcasted_iota(jnp.int32, (tok, wide * tok), 1), tok)
        causal = lax.broadcasted_iota(jnp.int32, (tok, wide * tok), 0) <= query_index
        for a in range(heads):
            for j in range(count - 1):
                arrival(kv.at[a, j], kv_recv.at[a, j]).wait_recv()
            loads[2 * a].wait()
            loads[2 * a + 1].wait()
            keys = kv[a, 0:count, 0].reshape(size, HD)
            values = kv[a, 0:count, 1].reshape(size, HD)
            keys_t = keys.T
            values_t = values.T
            for p in range(group // wide):
                first = a * group + p * wide
                queries = stacked(qbuf, first, wide)
                cotangents = stacked(gbuf, first, wide)
                raw = dot_nt(keys, queries)
                if count <= devices - reach:
                    raw = jnp.where(base * tok + key_index >= start_ref[0:1, :], raw, NEGATIVE)
                last = jnp.where(causal, raw[size - tok :], NEGATIVE)
                raw = jnp.concatenate([raw[: size - tok], last], axis=0) if count > 1 else last
                rowmax = jnp.max(raw, axis=0, keepdims=True)
                expo = jnp.exp2((raw - rowmax) * to_exp2)
                dprob = dot_nt(values, cotangents)
                inverse = 1.0 / jnp.sum(expo, axis=0, keepdims=True)
                delta = jnp.sum(expo * dprob, axis=0, keepdims=True) * inverse
                prob = expo * inverse
                prob_low = prob.astype(jnp.bfloat16)
                dscore = (prob * (dprob - delta)).astype(jnp.bfloat16)
                wide_cols = slice(p * wide * tok, (p + 1) * wide * tok)
                probs[0:size, wide_cols] = prob_low
                dscores[0:size, wide_cols] = dscore
                out = dot_nn(values_t, prob_low)
                grad = scale * dot_nn(keys_t, dscore)
                for h in range(wide):
                    cols = slice((first + h) * HD, (first + h + 1) * HD)
                    part = slice(h * tok, (h + 1) * tok)
                    ostage[:, cols] = out[:, part].T.astype(jnp.bfloat16)
                    qstage[:, cols] = grad[:, part].T.astype(jnp.bfloat16)
            key_part = dot_nn(dscores[0:size, :], stacked(qbuf, a * group, group))
            value_part = dot_nn(probs[0:size, :], stacked(gbuf, a * group, group))
            for j in range(count - 1):
                piece = slice(j * tok, (j + 1) * tok)
                gsend[a, j, 0] = key_part[piece].astype(jnp.bfloat16)
                gsend[a, j, 1] = value_part[piece].astype(jnp.bfloat16)
                (g_to_relay if count == reach and j in relayed else g_copy)(a, j).start()
            gown[a, 0] = key_part[size - tok :]
            gown[a, 1] = value_part[size - tok :]

    def any_count(sbuf, dbuf, oacc, qacc, rowmax, rowsum, delta):
        key_index = lax.broadcasted_iota(jnp.int32, (tok, tok), 0)
        query_index = lax.broadcasted_iota(jnp.int32, (tok, tok), 1)
        for a in range(heads):
            loads[2 * a].wait()
            loads[2 * a + 1].wait()
            queries = stacked(qbuf, a * group, group)
            cotangents = stacked(gbuf, a * group, group)
            rowmax[...] = jnp.full(rowmax.shape, NEGATIVE, jnp.float32)
            rowsum[...] = jnp.zeros(rowsum.shape, jnp.float32)
            delta[...] = jnp.zeros(delta.shape, jnp.float32)
            oacc[...] = jnp.zeros(oacc.shape, jnp.float32)
            qacc[...] = jnp.zeros(qacc.shape, jnp.float32)

            def first_pass(j, diagonal):
                allowed = (base + j) * tok + key_index >= start_ref[0:1, 0:tok]
                if diagonal:
                    allowed = allowed & (key_index <= query_index)
                raw = dot_nt(kv[a, j, 0], queries)
                for h in range(group):
                    cols = slice(h * tok, (h + 1) * tok)
                    masked = jnp.where(allowed, raw[:, cols], NEGATIVE)
                    sbuf[j, :, cols] = masked
                    rowmax[:, cols] = jnp.maximum(
                        rowmax[:, cols], jnp.max(masked, axis=0, keepdims=True)
                    )

            def first_step(j, _):
                arrival(kv.at[a, j], kv_recv.at[a, j]).wait_recv()
                first_pass(j, False)
                return 0

            first_pass(local, True)
            lax.fori_loop(0, local, first_step, 0)

            def second_step(j, _):
                dprob = dot_nt(kv[a, j, 1], cotangents)
                expo = jnp.exp2((sbuf[j] - rowmax[...]) * to_exp2)
                sbuf[j] = expo
                dbuf[j] = dprob
                rowsum[...] += jnp.sum(expo, axis=0, keepdims=True)
                delta[...] += jnp.sum(expo * dprob, axis=0, keepdims=True)
                return 0

            lax.fori_loop(0, local + 1, second_step, 0)
            rowsum[...] = 1.0 / rowsum[...]
            delta[...] = delta[...] * rowsum[...]

            def third_pass(j):
                prob = sbuf[j] * rowsum[...]
                prob_low = prob.astype(jnp.bfloat16)
                dscore = (prob * (dbuf[j] - delta[...])).astype(jnp.bfloat16)
                oacc[...] += dot_nn(kv[a, j, 1].T, prob_low)
                qacc[...] += dot_nn(kv[a, j, 0].T, dscore)
                return dot_nn(dscore, queries), dot_nn(prob_low, cotangents)

            def third_step(j, _):
                key_part, value_part = third_pass(j)
                gsend[a, j, 0] = key_part.astype(jnp.bfloat16)
                gsend[a, j, 1] = value_part.astype(jnp.bfloat16)
                g_copy(a, j).start()
                return 0

            lax.fori_loop(0, local, third_step, 0)
            gown[a, 0], gown[a, 1] = third_pass(local)
            for h in range(group):
                cols = slice((a * group + h) * HD, (a * group + h + 1) * HD)
                part = slice(h * tok, (h + 1) * tok)
                ostage[:, cols] = oacc[:, part].T.astype(jnp.bfloat16)
                qstage[:, cols] = (scale * qacc[:, part]).T.astype(jnp.bfloat16)

    if loop_refs:
        any_count(*loop_refs)
    else:
        for count in range(1, reach + 1):
            pl.when(local + 1 == count)(functools.partial(one_count, count))

    stores = [
        pltpu.make_async_copy(ostage, att_hbm, store_sem.at[0]),
        pltpu.make_async_copy(qstage, gq_hbm, store_sem.at[1]),
    ]
    for copy in stores:
        copy.start()

    if relaying:

        @pl.when(idx == reach)
        def _():
            for a in range(heads):
                for j in relayed:
                    g_to_relay(a, j).wait_recv()
                    g_forward(a, j).start()

    for a in range(heads):

        def collect(j, _, a=a):
            arrival(grecv.at[a, j], g_recv.at[a, j]).wait_recv()
            gown[a] += grecv[a, j].astype(jnp.float32)
            return 0

        lax.fori_loop(local + 1, after, collect, 0)
        cols = slice(a * HD, (a + 1) * HD)
        gk_ref[:, cols] = (scale * gown[a, 0]).astype(jnp.bfloat16)
        gv_ref[:, cols] = gown[a, 1].astype(jnp.bfloat16)

    for copy in stores:
        copy.wait()

    def end_l(target, _):
        @pl.when(target != idx)
        def _():
            l_copy(target).wait_send()

        return 0

    lax.fori_loop(reach, devices, end_l, 0)
    for a in range(heads):

        def end_kv(target, _, a=a):
            kv_copy(a, target).wait_send()
            return 0

        def end_g(j, _, a=a):
            g_copy(a, j).wait_send()
            return 0

        for j in relayed:
            pl.when(idx == j)(kv_to_relay(a, j).wait_send)
        lax.fori_loop(local + 1, after - skip, end_kv, 0)
        if not relaying:
            lax.fori_loop(0, local, end_g, 0)
            continue

        @pl.when(idx != reach - 1)
        def _(end_g=end_g):
            lax.fori_loop(0, local, end_g, 0)

        @pl.when(idx == reach - 1)
        def _(a=a):
            for j in range(reach - 1):
                (g_to_relay if j in relayed else g_copy)(a, j).wait_send()

        @pl.when(idx == reach)
        def _(a=a):
            for j in relayed:
                kv_forward(a, j).wait_send()
                g_forward(a, j).wait_send()


def hand_on(pieces, *refs):
    sources, targets, buffers = refs[0:4], refs[4:8], refs[8:12]
    in_sem, out_sem = refs[12:]
    copies = []
    for n in range(4):
        size = sources[n].shape[0] // pieces[n]
        for m in range(pieces[n]):
            part = pl.ds(m * size, size)
            copies.append(
                (
                    pltpu.make_async_copy(
                        sources[n].at[part], buffers[n].at[part], in_sem.at[n, m]
                    ),
                    pltpu.make_async_copy(
                        buffers[n].at[part], targets[n].at[part], out_sem.at[n, m]
                    ),
                )
            )
    for first, _ in copies:
        first.start()
    for first, second in copies:
        first.wait()
        second.start()
    for _, second in copies:
        second.wait()


def shards(query_rows, key_rows, value_rows, grad_out, lengths):
    tok, width = query_rows.shape
    heads = key_rows.shape[1] // HD
    group = width // HD // heads
    devices = lax.axis_size("seq")
    reach = devices // 2 + 1
    rows = group * tok
    docs = -(-lengths.shape[0] // 8) * 8
    wide = 2 if group % 2 == 0 else 1
    unrolled = reach <= UNROLLED
    relays = reach if unrolled else 1
    held = reach * tok if unrolled else 16
    anywhere = pl.BlockSpec(memory_space=pl.ANY)
    vmem = pl.BlockSpec(memory_space=pltpu.VMEM)
    dma = pltpu.SemaphoreType.DMA
    bf16, f32 = jnp.bfloat16, jnp.float32
    loop_scratch = [
        pltpu.VMEM((reach, tok, rows), f32),
        pltpu.VMEM((reach, tok, rows), f32),
        pltpu.VMEM((HD, rows), f32),
        pltpu.VMEM((HD, rows), f32),
        pltpu.VMEM((1, rows), f32),
        pltpu.VMEM((1, rows), f32),
        pltpu.VMEM((1, rows), f32),
    ]
    pairs = reach * rows * tok * heads
    shapes = (
        jax.ShapeDtypeStruct(query_rows.shape, bf16),
        jax.ShapeDtypeStruct(query_rows.shape, bf16),
        jax.ShapeDtypeStruct(key_rows.shape, bf16),
        jax.ShapeDtypeStruct(value_rows.shape, bf16),
    )
    pieces = (4, 4, 1, 1) if tok % 64 == 0 else (1, 1, 1, 1)
    results = pl.pallas_call(
        functools.partial(kernel, devices),
        out_shape=shapes,
        in_specs=[pl.BlockSpec(memory_space=pltpu.HBM)] * 4
        + [pl.BlockSpec(memory_space=pltpu.SMEM)],
        out_specs=(anywhere, anywhere, vmem, vmem),
        scratch_shapes=[
            pltpu.VMEM((tok, width), bf16),
            pltpu.VMEM((tok, width), bf16),
            pltpu.VMEM((heads, reach, 2, tok, HD), bf16),
            pltpu.VMEM((held, rows), bf16),
            pltpu.VMEM((held, rows), bf16),
            pltpu.VMEM((tok, width), bf16),
            pltpu.VMEM((tok, width), bf16),
            pltpu.VMEM((heads, reach, 2, tok, HD), bf16),
            pltpu.VMEM((heads, reach, 2, tok, HD), bf16),
            pltpu.VMEM((heads, 2, tok, HD), f32),
            pltpu.VMEM((devices, docs, HD), jnp.int32),
            pltpu.VMEM((1, wide * tok), jnp.int32),
            dma((heads, 2)),
            dma((heads, 2)),
            dma((2,)),
            dma((heads, reach)),
            dma((heads, reach)),
            dma((heads, reach)),
            dma((heads, reach)),
            dma((devices,)),
            dma((devices,)),
            pltpu.VMEM((heads, relays, 2, tok, HD), bf16),
            pltpu.VMEM((heads, relays, 2, tok, HD), bf16),
            dma((heads,)),
            dma((heads, relays)),
            dma((heads, relays)),
            dma((heads, relays)),
            dma((heads, relays)),
            dma((heads, relays)),
        ]
        + ([] if unrolled else loop_scratch),
        compiler_params=pltpu.CompilerParams(
            collective_id=0, has_side_effects=True, vmem_limit_bytes=(24 if unrolled else 56) * 1024 * 1024
        ),
        cost_estimate=pl.CostEstimate(
            flops=12 * pairs * HD, bytes_accessed=8 * tok * width, transcendentals=pairs
        ),
    )(query_rows, key_rows, value_rows, grad_out, lengths)
    return pl.pallas_call(
        functools.partial(hand_on, pieces),
        out_shape=shapes,
        in_specs=[anywhere] * 4,
        out_specs=(anywhere,) * 4,
        scratch_shapes=[pltpu.VMEM(shape.shape, bf16) for shape in shapes]
        + [dma((4, 4)), dma((4, 4))],
        cost_estimate=pl.CostEstimate(
            flops=0, bytes_accessed=8 * tok * width, transcendentals=0
        ),
    )(*results)


def solution(mesh):
    split = P(("groups", "seq"), "head")
    return jax.shard_map(
        shards,
        mesh=mesh,
        in_specs=(split, split, split, split, P(("groups", "seq"))),
        out_specs=(split, split, split, split),
        check_vma=False,
    )
```

```python
import functools
import math

import jax
import jax.numpy as jnp
from jax import lax
from jax.experimental import pallas as pl
from jax.experimental.pallas import tpu as pltpu
from jax.sharding import PartitionSpec as P

HD = 128
NEGATIVE = -1e30
MESH = pl.DeviceIdType.MESH
UNROLLED = 8


def dot_nt(a, b):
    return lax.dot_general(a, b, (((1,), (1,)), ((), ())), preferred_element_type=jnp.float32)


def dot_nn(a, b):
    return lax.dot_general(a, b, (((1,), (0,)), ((), ())), preferred_element_type=jnp.float32)


def stacked(ref, first, count):
    return ref[pl.ds(first, count)].reshape(count * ref.shape[1], HD)


def kernel(
    devices,
    q_hbm,
    k_hbm,
    v_hbm,
    g_hbm,
    len_ref,
    att_hbm,
    gq_hbm,
    gk_ref,
    gv_ref,
    qbuf,
    gbuf,
    kv,
    probs,
    dscores,
    ostage,
    qstage,
    gsend,
    grecv,
    gown,
    lens,
    start_ref,
    load_sem,
    kv_sem,
    store_sem,
    kv_send,
    kv_recv,
    g_send,
    g_recv,
    l_send,
    l_recv,
    *loop_refs,
):
    heads, reach, _, tok, _ = kv.shape
    group = qbuf.shape[0] // heads
    docs = len_ref.shape[0]
    scale = 1.0 / math.sqrt(HD)
    to_exp2 = scale * math.log2(math.e)
    wide = 2 if group % 2 == 0 else 1

    idx = lax.axis_index("seq")
    in_first = idx < reach
    base = jnp.where(in_first, 0, reach)
    local = idx - base
    after = jnp.where(in_first, reach, devices) - base

    own = []
    for a in range(heads):
        for n, source in enumerate((k_hbm, v_hbm)):
            own.append(
                pltpu.make_async_copy(
                    source.at[:, pl.ds(a * HD, HD)], kv.at[a, local, n], kv_sem.at[a, n]
                )
            )
    for copy in own:
        copy.start()

    def load(n, head):
        source, target = ((q_hbm, qbuf), (g_hbm, gbuf))[n]
        cols = pl.ds(pl.multiple_of(head * HD, HD), HD)
        return pltpu.make_async_copy(source.at[:, cols], target.at[head], load_sem.at[n, head])

    def save(n, head):
        source, target = ((ostage, att_hbm), (qstage, gq_hbm))[n]
        cols = pl.ds(pl.multiple_of(head * HD, HD), HD)
        return pltpu.make_async_copy(source.at[head], target.at[:, cols], store_sem.at[n, head])

    def for_heads(first, count, do):
        def step(head, _):
            do(0, head)
            do(1, head)
            return 0

        lax.fori_loop(first, first + count, step, 0)

    for_heads(0, heads * group, lambda n, head: load(n, head).start())

    barrier = pltpu.get_barrier_semaphore()

    def greet(step, _):
        other = lax.rem(idx + step, devices)
        pl.semaphore_signal(barrier, inc=1, device_id={"seq": other}, device_id_type=MESH)
        return 0

    lax.fori_loop(1, devices, greet, 0)

    lens[idx] = jnp.zeros(lens.shape[1:], jnp.int32)
    for n in range(docs):
        lens[idx, n : n + 1, :] = jnp.full((1, HD), len_ref[n], jnp.int32)
    start_ref[...] = jnp.zeros(start_ref.shape, jnp.int32)
    for copy in own:
        copy.wait()
    pl.semaphore_wait(barrier, devices - 1)

    def l_copy(target):
        return pltpu.make_async_remote_copy(
            src_ref=lens.at[idx],
            dst_ref=lens.at[idx],
            send_sem=l_send.at[target],
            recv_sem=l_recv.at[idx],
            device_id={"seq": target},
            device_id_type=MESH,
        )

    def kv_copy(a, target):
        return pltpu.make_async_remote_copy(
            src_ref=kv.at[a, local],
            dst_ref=kv.at[a, local],
            send_sem=kv_send.at[a, target],
            recv_sem=kv_recv.at[a, local],
            device_id={"seq": base + target},
            device_id_type=MESH,
        )

    def g_copy(a, j):
        return pltpu.make_async_remote_copy(
            src_ref=gsend.at[a, j],
            dst_ref=grecv.at[a, local],
            send_sem=g_send.at[a, j],
            recv_sem=g_recv.at[a, local],
            device_id={"seq": base + j},
            device_id_type=MESH,
        )

    def arrival(buf, sem):
        return pltpu.make_async_remote_copy(
            src_ref=buf,
            dst_ref=buf,
            send_sem=sem,
            recv_sem=sem,
            device_id={"seq": idx},
            device_id_type=MESH,
        )

    def start_l(target, _):
        @pl.when(target != idx)
        def _():
            l_copy(target).start()

        return 0

    lax.fori_loop(reach, devices, start_l, 0)
    for a in range(heads):

        def start_kv(n, _, a=a):
            kv_copy(a, after - 1 - n).start()
            return 0

        lax.fori_loop(0, after - 1 - local, start_kv, 0)

    @pl.when(jnp.logical_not(in_first))
    def _():
        position = idx * tok + lax.broadcasted_iota(jnp.int32, (1, tok), 1)

        def one(source, carry):
            @pl.when(source != idx)
            def _():
                arrival(lens.at[source], l_recv.at[source]).wait_recv()

            total, first = carry
            for n in range(docs):
                total = total + lens[source, n : n + 1, :]
                first = jnp.where(total <= position, total, first)
            return total, first

        zero = jnp.zeros((1, tok), jnp.int32)
        _, first = lax.fori_loop(0, devices, one, (zero, zero))
        for h in range(wide):
            start_ref[0:1, h * tok : (h + 1) * tok] = first

    def one_count(count):
        size = count * tok
        key_index = lax.broadcasted_iota(jnp.int32, (size, wide * tok), 0)
        query_index = lax.rem(lax.broadcasted_iota(jnp.int32, (tok, wide * tok), 1), tok)
        causal = lax.broadcasted_iota(jnp.int32, (tok, wide * tok), 0) <= query_index

        def one_head(a, _):
            for j in range(count - 1):
                arrival(kv.at[a, j], kv_recv.at[a, j]).wait_recv()
            for_heads(a * group, group, lambda n, head: load(n, head).wait())
            keys = kv[a, 0:count, 0].reshape(size, HD)
            values = kv[a, 0:count, 1].reshape(size, HD)
            keys_t = keys.T
            values_t = values.T

            def one_part(p, _):
                first = a * group + p * wide
                queries = stacked(qbuf, first, wide)
                cotangents = stacked(gbuf, first, wide)
                raw = dot_nt(keys, queries)
                if count <= devices - reach:
                    raw = jnp.where(base * tok + key_index >= start_ref[0:1, :], raw, NEGATIVE)
                last = jnp.where(causal, raw[size - tok :], NEGATIVE)
                raw = jnp.concatenate([raw[: size - tok], last], axis=0) if count > 1 else last
                rowmax = jnp.max(raw, axis=0, keepdims=True)
                expo = jnp.exp2((raw - rowmax) * to_exp2)
                dprob = dot_nt(values, cotangents)
                inverse = 1.0 / jnp.sum(expo, axis=0, keepdims=True)
                delta = jnp.sum(expo * dprob, axis=0, keepdims=True) * inverse
                prob = expo * inverse
                prob_low = prob.astype(jnp.bfloat16)
                dscore = (prob * (dprob - delta)).astype(jnp.bfloat16)
                cols = pl.ds(pl.multiple_of(p * wide * tok, wide * tok), wide * tok)
                probs[0:size, cols] = prob_low
                dscores[0:size, cols] = dscore
                out = dot_nn(values_t, prob_low)
                grad = scale * dot_nn(keys_t, dscore)
                for h in range(wide):
                    part = slice(h * tok, (h + 1) * tok)
                    ostage[first + h] = out[:, part].T.astype(jnp.bfloat16)
                    qstage[first + h] = grad[:, part].T.astype(jnp.bfloat16)
                return 0

            lax.fori_loop(0, group // wide, one_part, 0, unroll=2 if group // wide % 2 == 0 else 1)
            key_part = dot_nn(dscores[0:size, :], stacked(qbuf, a * group, group))
            value_part = dot_nn(probs[0:size, :], stacked(gbuf, a * group, group))
            for j in range(count - 1):
                piece = slice(j * tok, (j + 1) * tok)
                gsend[a, j, 0] = key_part[piece].astype(jnp.bfloat16)
                gsend[a, j, 1] = value_part[piece].astype(jnp.bfloat16)
                g_copy(a, j).start()
            gown[a, 0] = key_part[size - tok :]
            gown[a, 1] = value_part[size - tok :]
            for_heads(a * group, group, lambda n, head: save(n, head).start())
            return 0

        lax.fori_loop(0, heads, one_head, 0)

    def any_count(sbuf, dbuf, oacc, qacc, rowmax, rowsum, delta):
        key_index = lax.broadcasted_iota(jnp.int32, (tok, tok), 0)
        query_index = lax.broadcasted_iota(jnp.int32, (tok, tok), 1)
        for a in range(heads):
            for_heads(a * group, group, lambda n, head: load(n, head).wait())
            queries = stacked(qbuf, a * group, group)
            cotangents = stacked(gbuf, a * group, group)
            rowmax[...] = jnp.full(rowmax.shape, NEGATIVE, jnp.float32)
            rowsum[...] = jnp.zeros(rowsum.shape, jnp.float32)
            delta[...] = jnp.zeros(delta.shape, jnp.float32)
            oacc[...] = jnp.zeros(oacc.shape, jnp.float32)
            qacc[...] = jnp.zeros(qacc.shape, jnp.float32)

            def first_pass(j, diagonal):
                allowed = (base + j) * tok + key_index >= start_ref[0:1, 0:tok]
                if diagonal:
                    allowed = allowed & (key_index <= query_index)
                raw = dot_nt(kv[a, j, 0], queries)
                for h in range(group):
                    cols = slice(h * tok, (h + 1) * tok)
                    masked = jnp.where(allowed, raw[:, cols], NEGATIVE)
                    sbuf[j, :, cols] = masked
                    rowmax[:, cols] = jnp.maximum(
                        rowmax[:, cols], jnp.max(masked, axis=0, keepdims=True)
                    )

            def first_step(j, _):
                arrival(kv.at[a, j], kv_recv.at[a, j]).wait_recv()
                first_pass(j, False)
                return 0

            first_pass(local, True)
            lax.fori_loop(0, local, first_step, 0)

            def second_step(j, _):
                dprob = dot_nt(kv[a, j, 1], cotangents)
                expo = jnp.exp2((sbuf[j] - rowmax[...]) * to_exp2)
                sbuf[j] = expo
                dbuf[j] = dprob
                rowsum[...] += jnp.sum(expo, axis=0, keepdims=True)
                delta[...] += jnp.sum(expo * dprob, axis=0, keepdims=True)
                return 0

            lax.fori_loop(0, local + 1, second_step, 0)
            rowsum[...] = 1.0 / rowsum[...]
            delta[...] = delta[...] * rowsum[...]

            def third_pass(j):
                prob = sbuf[j] * rowsum[...]
                prob_low = prob.astype(jnp.bfloat16)
                dscore = (prob * (dbuf[j] - delta[...])).astype(jnp.bfloat16)
                oacc[...] += dot_nn(kv[a, j, 1].T, prob_low)
                qacc[...] += dot_nn(kv[a, j, 0].T, dscore)
                return dot_nn(dscore, queries), dot_nn(prob_low, cotangents)

            def third_step(j, _):
                key_part, value_part = third_pass(j)
                gsend[a, j, 0] = key_part.astype(jnp.bfloat16)
                gsend[a, j, 1] = value_part.astype(jnp.bfloat16)
                g_copy(a, j).start()
                return 0

            lax.fori_loop(0, local, third_step, 0)
            gown[a, 0], gown[a, 1] = third_pass(local)
            for h in range(group):
                part = slice(h * tok, (h + 1) * tok)
                ostage[a * group + h] = oacc[:, part].T.astype(jnp.bfloat16)
                qstage[a * group + h] = (scale * qacc[:, part]).T.astype(jnp.bfloat16)
            for_heads(a * group, group, lambda n, head: save(n, head).start())

    if loop_refs:
        any_count(*loop_refs)
    else:
        for count in range(1, reach + 1):
            pl.when(local + 1 == count)(functools.partial(one_count, count))

    for a in range(heads):

        def collect(j, _, a=a):
            arrival(grecv.at[a, j], g_recv.at[a, j]).wait_recv()
            gown[a] += grecv[a, j].astype(jnp.float32)
            return 0

        lax.fori_loop(local + 1, after, collect, 0)
        cols = slice(a * HD, (a + 1) * HD)
        gk_ref[:, cols] = (scale * gown[a, 0]).astype(jnp.bfloat16)
        gv_ref[:, cols] = gown[a, 1].astype(jnp.bfloat16)

    for_heads(0, heads * group, lambda n, head: save(n, head).wait())

    def end_l(target, _):
        @pl.when(target != idx)
        def _():
            l_copy(target).wait_send()

        return 0

    lax.fori_loop(reach, devices, end_l, 0)
    for a in range(heads):

        def end_kv(target, _, a=a):
            kv_copy(a, target).wait_send()
            return 0

        def end_g(j, _, a=a):
            g_copy(a, j).wait_send()
            return 0

        lax.fori_loop(local + 1, after, end_kv, 0)
        lax.fori_loop(0, local, end_g, 0)


def hand_on(pieces, *refs):
    sources, targets, buffers = refs[0:4], refs[4:8], refs[8:12]
    in_sem, out_sem = refs[12:]
    copies = []
    for n in range(4):
        size = sources[n].shape[0] // pieces[n]
        for m in range(pieces[n]):
            part = pl.ds(m * size, size)
            copies.append(
                (
                    pltpu.make_async_copy(
                        sources[n].at[part], buffers[n].at[part], in_sem.at[n, m]
                    ),
                    pltpu.make_async_copy(
                        buffers[n].at[part], targets[n].at[part], out_sem.at[n, m]
                    ),
                )
            )
    for first, _ in copies:
        first.start()
    for first, second in copies:
        first.wait()
        second.start()
    for _, second in copies:
        second.wait()


def shards(query_rows, key_rows, value_rows, grad_out, lengths):
    tok, width = query_rows.shape
    heads = key_rows.shape[1] // HD
    group = width // HD // heads
    devices = lax.axis_size("seq")
    reach = devices // 2 + 1
    rows = group * tok
    docs = -(-lengths.shape[0] // 8) * 8
    wide = 2 if group % 2 == 0 else 1
    unrolled = reach <= UNROLLED
    held = reach * tok if unrolled else 16
    anywhere = pl.BlockSpec(memory_space=pl.ANY)
    vmem = pl.BlockSpec(memory_space=pltpu.VMEM)
    dma = pltpu.SemaphoreType.DMA
    bf16, f32 = jnp.bfloat16, jnp.float32
    loop_scratch = [
        pltpu.VMEM((reach, tok, rows), f32),
        pltpu.VMEM((reach, tok, rows), f32),
        pltpu.VMEM((HD, rows), f32),
        pltpu.VMEM((HD, rows), f32),
        pltpu.VMEM((1, rows), f32),
        pltpu.VMEM((1, rows), f32),
        pltpu.VMEM((1, rows), f32),
    ]
    pairs = reach * rows * tok * heads
    shapes = (
        jax.ShapeDtypeStruct(query_rows.shape, bf16),
        jax.ShapeDtypeStruct(query_rows.shape, bf16),
        jax.ShapeDtypeStruct(key_rows.shape, bf16),
        jax.ShapeDtypeStruct(value_rows.shape, bf16),
    )
    pieces = (4, 4, 1, 1) if tok % 64 == 0 else (1, 1, 1, 1)
    results = pl.pallas_call(
        functools.partial(kernel, devices),
        out_shape=shapes,
        in_specs=[anywhere] * 4 + [pl.BlockSpec(memory_space=pltpu.SMEM)],
        out_specs=(anywhere, anywhere, vmem, vmem),
        scratch_shapes=[
            pltpu.VMEM((heads * group, tok, HD), bf16),
            pltpu.VMEM((heads * group, tok, HD), bf16),
            pltpu.VMEM((heads, reach, 2, tok, HD), bf16),
            pltpu.VMEM((held, rows), bf16),
            pltpu.VMEM((held, rows), bf16),
            pltpu.VMEM((heads * group, tok, HD), bf16),
            pltpu.VMEM((heads * group, tok, HD), bf16),
            pltpu.VMEM((heads, reach, 2, tok, HD), bf16),
            pltpu.VMEM((heads, reach, 2, tok, HD), bf16),
            pltpu.VMEM((heads, 2, tok, HD), f32),
            pltpu.VMEM((devices, docs, HD), jnp.int32),
            pltpu.VMEM((1, wide * tok), jnp.int32),
            dma((2, heads * group)),
            dma((heads, 2)),
            dma((2, heads * group)),
            dma((heads, reach)),
            dma((heads, reach)),
            dma((heads, reach)),
            dma((heads, reach)),
            dma((devices,)),
            dma((devices,)),
        ]
        + ([] if unrolled else loop_scratch),
        compiler_params=pltpu.CompilerParams(
            collective_id=0, has_side_effects=True, vmem_limit_bytes=56 * 1024 * 1024
        ),
        cost_estimate=pl.CostEstimate(
            flops=12 * pairs * HD, bytes_accessed=8 * tok * width, transcendentals=pairs
        ),
    )(query_rows, key_rows, value_rows, grad_out, lengths)
    return pl.pallas_call(
        functools.partial(hand_on, pieces),
        out_shape=shapes,
        in_specs=[anywhere] * 4,
        out_specs=(anywhere,) * 4,
        scratch_shapes=[pltpu.VMEM(shape.shape, bf16) for shape in shapes]
        + [dma((4, 4)), dma((4, 4))],
        cost_estimate=pl.CostEstimate(
            flops=0, bytes_accessed=8 * tok * width, transcendentals=0
        ),
    )(*results)


def solution(mesh):
    split = P(("groups", "seq"), "head")
    return jax.shard_map(
        shards,
        mesh=mesh,
        in_specs=(split, split, split, split, P(("groups", "seq"))),
        out_specs=(split, split, split, split),
        check_vma=False,
    )
```

```python
import functools
import math

import jax
import jax.numpy as jnp
from jax import lax
from jax.experimental import pallas as pl
from jax.experimental.pallas import tpu as pltpu
from jax.sharding import PartitionSpec as P

HD = 128
NEGATIVE = -1e30
MESH = pl.DeviceIdType.MESH
UNROLLED = 8


def dot_nt(a, b):
    return lax.dot_general(a, b, (((1,), (1,)), ((), ())), preferred_element_type=jnp.float32)


def dot_nn(a, b):
    return lax.dot_general(a, b, (((1,), (0,)), ((), ())), preferred_element_type=jnp.float32)


def stacked(ref, first, count):
    return jnp.concatenate(
        [ref[:, (first + h) * HD : (first + h + 1) * HD] for h in range(count)], axis=0
    )


def kernel(
    devices,
    q_hbm,
    k_hbm,
    v_hbm,
    g_hbm,
    len_ref,
    att_hbm,
    gq_hbm,
    gk_ref,
    gv_ref,
    qbuf,
    gbuf,
    kv,
    probs,
    dscores,
    ostage,
    qstage,
    gsend,
    grecv,
    gown,
    lens,
    start_ref,
    load_sem,
    kv_sem,
    store_sem,
    kv_send,
    kv_recv,
    g_send,
    g_recv,
    l_send,
    l_recv,
    *loop_refs,
):
    heads, reach, _, tok, _ = kv.shape
    group = qbuf.shape[1] // HD // heads
    docs = len_ref.shape[0]
    scale = 1.0 / math.sqrt(HD)
    to_exp2 = scale * math.log2(math.e)
    wide = 2 if group % 2 == 0 else 1

    idx = lax.axis_index("seq")
    in_first = idx < reach
    base = jnp.where(in_first, 0, reach)
    local = idx - base
    after = jnp.where(in_first, reach, devices) - base

    own = []
    for a in range(heads):
        for n, source in enumerate((k_hbm, v_hbm)):
            own.append(
                pltpu.make_async_copy(
                    source.at[:, pl.ds(a * HD, HD)], kv.at[a, local, n], kv_sem.at[a, n]
                )
            )
    loads = []
    for a in range(heads):
        cols = pl.ds(a * group * HD, group * HD)
        for n, (source, target) in enumerate(((q_hbm, qbuf), (g_hbm, gbuf))):
            loads.append(
                pltpu.make_async_copy(source.at[:, cols], target.at[:, cols], load_sem.at[a, n])
            )
    for copy in own + loads:
        copy.start()

    barrier = pltpu.get_barrier_semaphore()

    def greet(step, _):
        other = lax.rem(idx + step, devices)
        pl.semaphore_signal(barrier, inc=1, device_id={"seq": other}, device_id_type=MESH)
        return 0

    lax.fori_loop(1, devices, greet, 0)

    lens[idx] = jnp.zeros(lens.shape[1:], jnp.int32)
    for n in range(docs):
        lens[idx, n : n + 1, :] = jnp.full((1, HD), len_ref[n], jnp.int32)
    start_ref[...] = jnp.zeros(start_ref.shape, jnp.int32)
    for copy in own:
        copy.wait()
    pl.semaphore_wait(barrier, devices - 1)

    def l_copy(target):
        return pltpu.make_async_remote_copy(
            src_ref=lens.at[idx],
            dst_ref=lens.at[idx],
            send_sem=l_send.at[target],
            recv_sem=l_recv.at[idx],
            device_id={"seq": target},
            device_id_type=MESH,
        )

    def kv_copy(a, target):
        return pltpu.make_async_remote_copy(
            src_ref=kv.at[a, local],
            dst_ref=kv.at[a, local],
            send_sem=kv_send.at[a, target],
            recv_sem=kv_recv.at[a, local],
            device_id={"seq": base + target},
            device_id_type=MESH,
        )

    def g_copy(a, j):
        return pltpu.make_async_remote_copy(
            src_ref=gsend.at[a, j],
            dst_ref=grecv.at[a, local],
            send_sem=g_send.at[a, j],
            recv_sem=g_recv.at[a, local],
            device_id={"seq": base + j},
            device_id_type=MESH,
        )

    def arrival(buf, sem):
        return pltpu.make_async_remote_copy(
            src_ref=buf,
            dst_ref=buf,
            send_sem=sem,
            recv_sem=sem,
            device_id={"seq": idx},
            device_id_type=MESH,
        )

    def start_l(target, _):
        @pl.when(target != idx)
        def _():
            l_copy(target).start()

        return 0

    lax.fori_loop(reach, devices, start_l, 0)
    for a in range(heads):

        def start_kv(n, _, a=a):
            kv_copy(a, after - 1 - n).start()
            return 0

        lax.fori_loop(0, after - 1 - local, start_kv, 0)

    @pl.when(jnp.logical_not(in_first))
    def _():
        position = idx * tok + lax.broadcasted_iota(jnp.int32, (1, tok), 1)

        def one(source, carry):
            @pl.when(source != idx)
            def _():
                arrival(lens.at[source], l_recv.at[source]).wait_recv()

            total, first = carry
            for n in range(docs):
                total = total + lens[source, n : n + 1, :]
                first = jnp.where(total <= position, total, first)
            return total, first

        zero = jnp.zeros((1, tok), jnp.int32)
        _, first = lax.fori_loop(0, devices, one, (zero, zero))
        for h in range(wide):
            start_ref[0:1, h * tok : (h + 1) * tok] = first

    def one_count(count):
        size = count * tok
        key_index = lax.broadcasted_iota(jnp.int32, (size, wide * tok), 0)
        query_index = lax.rem(lax.broadcasted_iota(jnp.int32, (tok, wide * tok), 1), tok)
        causal = lax.broadcasted_iota(jnp.int32, (tok, wide * tok), 0) <= query_index
        for a in range(heads):
            for j in range(count - 1):
                arrival(kv.at[a, j], kv_recv.at[a, j]).wait_recv()
            loads[2 * a].wait()
            loads[2 * a + 1].wait()
            keys = kv[a, 0:count, 0].reshape(size, HD)
            values = kv[a, 0:count, 1].reshape(size, HD)
            keys_t = keys.T
            values_t = values.T
            for p in range(group // wide):
                first = a * group + p * wide
                queries = stacked(qbuf, first, wide)
                cotangents = stacked(gbuf, first, wide)
                raw = dot_nt(keys, queries)
                if count <= devices - reach:
                    raw = jnp.where(base * tok + key_index >= start_ref[0:1, :], raw, NEGATIVE)
                last = jnp.where(causal, raw[size - tok :], NEGATIVE)
                raw = jnp.concatenate([raw[: size - tok], last], axis=0) if count > 1 else last
                rowmax = jnp.max(raw, axis=0, keepdims=True)
                expo = jnp.exp2((raw - rowmax) * to_exp2)
                dprob = dot_nt(values, cotangents)
                inverse = 1.0 / jnp.sum(expo, axis=0, keepdims=True)
                delta = jnp.sum(expo * dprob, axis=0, keepdims=True) * inverse
                prob = expo * inverse
                prob_low = prob.astype(jnp.bfloat16)
                dscore = (prob * (dprob - delta)).astype(jnp.bfloat16)
                wide_cols = slice(p * wide * tok, (p + 1) * wide * tok)
                probs[0:size, wide_cols] = prob_low
                dscores[0:size, wide_cols] = dscore
                out = dot_nn(values_t, prob_low).astype(jnp.bfloat16).T
                grad = (scale * dot_nn(keys_t, dscore)).astype(jnp.bfloat16).T
                for h in range(wide):
                    cols = slice((first + h) * HD, (first + h + 1) * HD)
                    part = slice(h * tok, (h + 1) * tok)
                    ostage[:, cols] = out[part]
                    qstage[:, cols] = grad[part]
            key_part = dot_nn(dscores[0:size, :], stacked(qbuf, a * group, group))
            value_part = dot_nn(probs[0:size, :], stacked(gbuf, a * group, group))
            for j in range(count - 1):
                piece = slice(j * tok, (j + 1) * tok)
                gsend[a, j, 0] = key_part[piece].astype(jnp.bfloat16)
                gsend[a, j, 1] = value_part[piece].astype(jnp.bfloat16)
                g_copy(a, j).start()
            gown[a, 0] = key_part[size - tok :]
            gown[a, 1] = value_part[size - tok :]

    def any_count(sbuf, dbuf, oacc, qacc, rowmax, rowsum, delta):
        key_index = lax.broadcasted_iota(jnp.int32, (tok, tok), 0)
        query_index = lax.broadcasted_iota(jnp.int32, (tok, tok), 1)
        for a in range(heads):
            loads[2 * a].wait()
            loads[2 * a + 1].wait()
            queries = stacked(qbuf, a * group, group)
            cotangents = stacked(gbuf, a * group, group)
            rowmax[...] = jnp.full(rowmax.shape, NEGATIVE, jnp.float32)
            rowsum[...] = jnp.zeros(rowsum.shape, jnp.float32)
            delta[...] = jnp.zeros(delta.shape, jnp.float32)
            oacc[...] = jnp.zeros(oacc.shape, jnp.float32)
            qacc[...] = jnp.zeros(qacc.shape, jnp.float32)

            def first_pass(j, diagonal):
                allowed = (base + j) * tok + key_index >= start_ref[0:1, 0:tok]
                if diagonal:
                    allowed = allowed & (key_index <= query_index)
                raw = dot_nt(kv[a, j, 0], queries)
                for h in range(group):
                    cols = slice(h * tok, (h + 1) * tok)
                    masked = jnp.where(allowed, raw[:, cols], NEGATIVE)
                    sbuf[j, :, cols] = masked
                    rowmax[:, cols] = jnp.maximum(
                        rowmax[:, cols], jnp.max(masked, axis=0, keepdims=True)
                    )

            def first_step(j, _):
                arrival(kv.at[a, j], kv_recv.at[a, j]).wait_recv()
                first_pass(j, False)
                return 0

            first_pass(local, True)
            lax.fori_loop(0, local, first_step, 0)

            def second_step(j, _):
                dprob = dot_nt(kv[a, j, 1], cotangents)
                expo = jnp.exp2((sbuf[j] - rowmax[...]) * to_exp2)
                sbuf[j] = expo
                dbuf[j] = dprob
                rowsum[...] += jnp.sum(expo, axis=0, keepdims=True)
                delta[...] += jnp.sum(expo * dprob, axis=0, keepdims=True)
                return 0

            lax.fori_loop(0, local + 1, second_step, 0)
            rowsum[...] = 1.0 / rowsum[...]
            delta[...] = delta[...] * rowsum[...]

            def third_pass(j):
                prob = sbuf[j] * rowsum[...]
                prob_low = prob.astype(jnp.bfloat16)
                dscore = (prob * (dbuf[j] - delta[...])).astype(jnp.bfloat16)
                oacc[...] += dot_nn(kv[a, j, 1].T, prob_low)
                qacc[...] += dot_nn(kv[a, j, 0].T, dscore)
                return dot_nn(dscore, queries), dot_nn(prob_low, cotangents)

            def third_step(j, _):
                key_part, value_part = third_pass(j)
                gsend[a, j, 0] = key_part.astype(jnp.bfloat16)
                gsend[a, j, 1] = value_part.astype(jnp.bfloat16)
                g_copy(a, j).start()
                return 0

            lax.fori_loop(0, local, third_step, 0)
            gown[a, 0], gown[a, 1] = third_pass(local)
            for h in range(group):
                cols = slice((a * group + h) * HD, (a * group + h + 1) * HD)
                part = slice(h * tok, (h + 1) * tok)
                ostage[:, cols] = oacc[:, part].T.astype(jnp.bfloat16)
                qstage[:, cols] = (scale * qacc[:, part]).T.astype(jnp.bfloat16)

    if loop_refs:
        any_count(*loop_refs)
    else:
        for count in range(1, reach + 1):
            pl.when(local + 1 == count)(functools.partial(one_count, count))

    stores = [
        pltpu.make_async_copy(ostage, att_hbm, store_sem.at[0]),
        pltpu.make_async_copy(qstage, gq_hbm, store_sem.at[1]),
    ]
    for copy in stores:
        copy.start()

    for a in range(heads):

        def collect(j, _, a=a):
            arrival(grecv.at[a, j], g_recv.at[a, j]).wait_recv()
            gown[a] += grecv[a, j].astype(jnp.float32)
            return 0

        lax.fori_loop(local + 1, after, collect, 0)
        cols = slice(a * HD, (a + 1) * HD)
        gk_ref[:, cols] = (scale * gown[a, 0]).astype(jnp.bfloat16)
        gv_ref[:, cols] = gown[a, 1].astype(jnp.bfloat16)

    for copy in stores:
        copy.wait()

    def end_l(target, _):
        @pl.when(target != idx)
        def _():
            l_copy(target).wait_send()

        return 0

    lax.fori_loop(reach, devices, end_l, 0)
    for a in range(heads):

        def end_kv(target, _, a=a):
            kv_copy(a, target).wait_send()
            return 0

        def end_g(j, _, a=a):
            g_copy(a, j).wait_send()
            return 0

        lax.fori_loop(local + 1, after, end_kv, 0)
        lax.fori_loop(0, local, end_g, 0)


def hand_on(pieces, *refs):
    sources, targets, buffers = refs[0:4], refs[4:8], refs[8:12]
    in_sem, out_sem = refs[12:]
    copies = []
    for n in range(4):
        size = sources[n].shape[0] // pieces[n]
        for m in range(pieces[n]):
            part = pl.ds(m * size, size)
            copies.append(
                (
                    pltpu.make_async_copy(
                        sources[n].at[part], buffers[n].at[part], in_sem.at[n, m]
                    ),
                    pltpu.make_async_copy(
                        buffers[n].at[part], targets[n].at[part], out_sem.at[n, m]
                    ),
                )
            )
    for first, _ in copies:
        first.start()
    for first, second in copies:
        first.wait()
        second.start()
    for _, second in copies:
        second.wait()


def shards(query_rows, key_rows, value_rows, grad_out, lengths):
    tok, width = query_rows.shape
    heads = key_rows.shape[1] // HD
    group = width // HD // heads
    devices = lax.axis_size("seq")
    reach = devices // 2 + 1
    rows = group * tok
    docs = -(-lengths.shape[0] // 8) * 8
    wide = 2 if group % 2 == 0 else 1
    unrolled = reach <= UNROLLED
    held = reach * tok if unrolled else 16
    anywhere = pl.BlockSpec(memory_space=pl.ANY)
    vmem = pl.BlockSpec(memory_space=pltpu.VMEM)
    dma = pltpu.SemaphoreType.DMA
    bf16, f32 = jnp.bfloat16, jnp.float32
    loop_scratch = [
        pltpu.VMEM((reach, tok, rows), f32),
        pltpu.VMEM((reach, tok, rows), f32),
        pltpu.VMEM((HD, rows), f32),
        pltpu.VMEM((HD, rows), f32),
        pltpu.VMEM((1, rows), f32),
        pltpu.VMEM((1, rows), f32),
        pltpu.VMEM((1, rows), f32),
    ]
    pairs = reach * rows * tok * heads
    shapes = (
        jax.ShapeDtypeStruct(query_rows.shape, bf16),
        jax.ShapeDtypeStruct(query_rows.shape, bf16),
        jax.ShapeDtypeStruct(key_rows.shape, bf16),
        jax.ShapeDtypeStruct(value_rows.shape, bf16),
    )
    pieces = (4, 4, 1, 1) if tok % 64 == 0 else (1, 1, 1, 1)
    results = pl.pallas_call(
        functools.partial(kernel, devices),
        out_shape=shapes,
        in_specs=[anywhere] * 4 + [pl.BlockSpec(memory_space=pltpu.SMEM)],
        out_specs=(anywhere, anywhere, vmem, vmem),
        scratch_shapes=[
            pltpu.VMEM((tok, width), bf16),
            pltpu.VMEM((tok, width), bf16),
            pltpu.VMEM((heads, reach, 2, tok, HD), bf16),
            pltpu.VMEM((held, rows), bf16),
            pltpu.VMEM((held, rows), bf16),
            pltpu.VMEM((tok, width), bf16),
            pltpu.VMEM((tok, width), bf16),
            pltpu.VMEM((heads, reach, 2, tok, HD), bf16),
            pltpu.VMEM((heads, reach, 2, tok, HD), bf16),
            pltpu.VMEM((heads, 2, tok, HD), f32),
            pltpu.VMEM((devices, docs, HD), jnp.int32),
            pltpu.VMEM((1, wide * tok), jnp.int32),
            dma((heads, 2)),
            dma((heads, 2)),
            dma((2,)),
            dma((heads, reach)),
            dma((heads, reach)),
            dma((heads, reach)),
            dma((heads, reach)),
            dma((devices,)),
            dma((devices,)),
        ]
        + ([] if unrolled else loop_scratch),
        compiler_params=pltpu.CompilerParams(
            collective_id=0, has_side_effects=True, vmem_limit_bytes=56 * 1024 * 1024
        ),
        cost_estimate=pl.CostEstimate(
            flops=12 * pairs * HD, bytes_accessed=8 * tok * width, transcendentals=pairs
        ),
    )(query_rows, key_rows, value_rows, grad_out, lengths)
    return pl.pallas_call(
        functools.partial(hand_on, pieces),
        out_shape=shapes,
        in_specs=[anywhere] * 4,
        out_specs=(anywhere,) * 4,
        scratch_shapes=[pltpu.VMEM(shape.shape, bf16) for shape in shapes]
        + [dma((4, 4)), dma((4, 4))],
        cost_estimate=pl.CostEstimate(
            flops=0, bytes_accessed=8 * tok * width, transcendentals=0
        ),
    )(*results)


def solution(mesh):
    split = P(("groups", "seq"), "head")
    return jax.shard_map(
        shards,
        mesh=mesh,
        in_specs=(split, split, split, split, P(("groups", "seq"))),
        out_specs=(split, split, split, split),
        check_vma=False,
    )
```

```python
import functools
import math

import jax
import jax.numpy as jnp
from jax import lax
from jax.experimental import pallas as pl
from jax.experimental.pallas import tpu as pltpu
from jax.sharding import PartitionSpec as P

HD = 128
NEGATIVE = -1e30
MESH = pl.DeviceIdType.MESH
UNROLLED = 8


def dot_nt(a, b):
    return lax.dot_general(a, b, (((1,), (1,)), ((), ())), preferred_element_type=jnp.float32)


def dot_nn(a, b):
    return lax.dot_general(a, b, (((1,), (0,)), ((), ())), preferred_element_type=jnp.float32)


def stacked(ref, first, count):
    return jnp.concatenate(
        [ref[:, (first + h) * HD : (first + h + 1) * HD] for h in range(count)], axis=0
    )


def kernel(
    devices,
    q_hbm,
    k_hbm,
    v_hbm,
    g_hbm,
    len_ref,
    att_hbm,
    gq_hbm,
    gk_ref,
    gv_ref,
    qbuf,
    gbuf,
    kv,
    probs,
    dscores,
    ostage,
    qstage,
    gsend,
    grecv,
    gown,
    lens,
    start_ref,
    load_sem,
    kv_sem,
    store_sem,
    kv_send,
    kv_recv,
    g_send,
    g_recv,
    l_send,
    l_recv,
    *loop_refs,
):
    heads, reach, _, tok, _ = kv.shape
    group = qbuf.shape[1] // HD // heads
    docs = len_ref.shape[0]
    scale = 1.0 / math.sqrt(HD)
    to_exp2 = scale * math.log2(math.e)
    wide = 4 if group % 4 == 0 else 1

    idx = lax.axis_index("seq")
    in_first = idx < reach
    base = jnp.where(in_first, 0, reach)
    local = idx - base
    after = jnp.where(in_first, reach, devices) - base

    own = []
    for a in range(heads):
        for n, source in enumerate((k_hbm, v_hbm)):
            own.append(
                pltpu.make_async_copy(
                    source.at[:, pl.ds(a * HD, HD)], kv.at[a, local, n], kv_sem.at[a, n]
                )
            )
    loads = []
    for a in range(heads):
        cols = pl.ds(a * group * HD, group * HD)
        for n, (source, target) in enumerate(((q_hbm, qbuf), (g_hbm, gbuf))):
            loads.append(
                pltpu.make_async_copy(source.at[:, cols], target.at[:, cols], load_sem.at[a, n])
            )
    for copy in own + loads:
        copy.start()

    barrier = pltpu.get_barrier_semaphore()

    def greet(step, _):
        other = lax.rem(idx + step, devices)
        pl.semaphore_signal(barrier, inc=1, device_id={"seq": other}, device_id_type=MESH)
        return 0

    lax.fori_loop(1, devices, greet, 0)

    lens[idx] = jnp.zeros(lens.shape[1:], jnp.int32)
    for n in range(docs):
        lens[idx, n : n + 1, :] = jnp.full((1, HD), len_ref[n], jnp.int32)
    start_ref[...] = jnp.zeros(start_ref.shape, jnp.int32)
    for copy in own:
        copy.wait()
    pl.semaphore_wait(barrier, devices - 1)

    def l_copy(target):
        return pltpu.make_async_remote_copy(
            src_ref=lens.at[idx],
            dst_ref=lens.at[idx],
            send_sem=l_send.at[target],
            recv_sem=l_recv.at[idx],
            device_id={"seq": target},
            device_id_type=MESH,
        )

    def kv_copy(a, target):
        return pltpu.make_async_remote_copy(
            src_ref=kv.at[a, local],
            dst_ref=kv.at[a, local],
            send_sem=kv_send.at[a, target],
            recv_sem=kv_recv.at[a, local],
            device_id={"seq": base + target},
            device_id_type=MESH,
        )

    def g_copy(a, j):
        return pltpu.make_async_remote_copy(
            src_ref=gsend.at[a, j],
            dst_ref=grecv.at[a, local],
            send_sem=g_send.at[a, j],
            recv_sem=g_recv.at[a, local],
            device_id={"seq": base + j},
            device_id_type=MESH,
        )

    def arrival(buf, sem):
        return pltpu.make_async_remote_copy(
            src_ref=buf,
            dst_ref=buf,
            send_sem=sem,
            recv_sem=sem,
            device_id={"seq": idx},
            device_id_type=MESH,
        )

    def start_l(target, _):
        @pl.when(target != idx)
        def _():
            l_copy(target).start()

        return 0

    lax.fori_loop(reach, devices, start_l, 0)
    for a in range(heads):

        def start_kv(n, _, a=a):
            kv_copy(a, after - 1 - n).start()
            return 0

        lax.fori_loop(0, after - 1 - local, start_kv, 0)

    @pl.when(jnp.logical_not(in_first))
    def _():
        position = idx * tok + lax.broadcasted_iota(jnp.int32, (1, tok), 1)

        def one(source, carry):
            @pl.when(source != idx)
            def _():
                arrival(lens.at[source], l_recv.at[source]).wait_recv()

            total, first = carry
            for n in range(docs):
                total = total + lens[source, n : n + 1, :]
                first = jnp.where(total <= position, total, first)
            return total, first

        zero = jnp.zeros((1, tok), jnp.int32)
        _, first = lax.fori_loop(0, devices, one, (zero, zero))
        for h in range(wide):
            start_ref[0:1, h * tok : (h + 1) * tok] = first

    def one_count(count):
        size = count * tok
        key_index = lax.broadcasted_iota(jnp.int32, (size, wide * tok), 0)
        query_index = lax.rem(lax.broadcasted_iota(jnp.int32, (tok, wide * tok), 1), tok)
        causal = lax.broadcasted_iota(jnp.int32, (tok, wide * tok), 0) <= query_index
        for a in range(heads):
            for j in range(count - 1):
                arrival(kv.at[a, j], kv_recv.at[a, j]).wait_recv()
            loads[2 * a].wait()
            loads[2 * a + 1].wait()
            keys = kv[a, 0:count, 0].reshape(size, HD)
            values = kv[a, 0:count, 1].reshape(size, HD)
            keys_t = keys.T
            values_t = values.T
            for p in range(group // wide):
                first = a * group + p * wide
                queries = stacked(qbuf, first, wide)
                cotangents = stacked(gbuf, first, wide)
                raw = dot_nt(keys, queries)
                if count <= devices - reach:
                    raw = jnp.where(base * tok + key_index >= start_ref[0:1, :], raw, NEGATIVE)
                last = jnp.where(causal, raw[size - tok :], NEGATIVE)
                raw = jnp.concatenate([raw[: size - tok], last], axis=0) if count > 1 else last
                rowmax = jnp.max(raw, axis=0, keepdims=True)
                expo = jnp.exp2((raw - rowmax) * to_exp2)
                dprob = dot_nt(values, cotangents)
                inverse = 1.0 / jnp.sum(expo, axis=0, keepdims=True)
                delta = jnp.sum(expo * dprob, axis=0, keepdims=True) * inverse
                prob = expo * inverse
                prob_low = prob.astype(jnp.bfloat16)
                dscore = (prob * (dprob - delta)).astype(jnp.bfloat16)
                wide_cols = slice(p * wide * tok, (p + 1) * wide * tok)
                probs[0:size, wide_cols] = prob_low
                dscores[0:size, wide_cols] = dscore
                out = dot_nn(values_t, prob_low).astype(jnp.bfloat16).T
                grad = (scale * dot_nn(keys_t, dscore)).astype(jnp.bfloat16).T
                for h in range(wide):
                    cols = slice((first + h) * HD, (first + h + 1) * HD)
                    part = slice(h * tok, (h + 1) * tok)
                    ostage[:, cols] = out[part]
                    qstage[:, cols] = grad[part]
            key_part = dot_nn(dscores[0:size, :], stacked(qbuf, a * group, group))
            value_part = dot_nn(probs[0:size, :], stacked(gbuf, a * group, group))
            for j in range(count - 1):
                piece = slice(j * tok, (j + 1) * tok)
                gsend[a, j, 0] = key_part[piece].astype(jnp.bfloat16)
                gsend[a, j, 1] = value_part[piece].astype(jnp.bfloat16)
                g_copy(a, j).start()
            gown[a, 0] = key_part[size - tok :]
            gown[a, 1] = value_part[size - tok :]

    def any_count(sbuf, dbuf, oacc, qacc, rowmax, rowsum, delta):
        key_index = lax.broadcasted_iota(jnp.int32, (tok, tok), 0)
        query_index = lax.broadcasted_iota(jnp.int32, (tok, tok), 1)
        for a in range(heads):
            loads[2 * a].wait()
            loads[2 * a + 1].wait()
            queries = stacked(qbuf, a * group, group)
            cotangents = stacked(gbuf, a * group, group)
            rowmax[...] = jnp.full(rowmax.shape, NEGATIVE, jnp.float32)
            rowsum[...] = jnp.zeros(rowsum.shape, jnp.float32)
            delta[...] = jnp.zeros(delta.shape, jnp.float32)
            oacc[...] = jnp.zeros(oacc.shape, jnp.float32)
            qacc[...] = jnp.zeros(qacc.shape, jnp.float32)

            def first_pass(j, diagonal):
                allowed = (base + j) * tok + key_index >= start_ref[0:1, 0:tok]
                if diagonal:
                    allowed = allowed & (key_index <= query_index)
                raw = dot_nt(kv[a, j, 0], queries)
                for h in range(group):
                    cols = slice(h * tok, (h + 1) * tok)
                    masked = jnp.where(allowed, raw[:, cols], NEGATIVE)
                    sbuf[j, :, cols] = masked
                    rowmax[:, cols] = jnp.maximum(
                        rowmax[:, cols], jnp.max(masked, axis=0, keepdims=True)
                    )

            def first_step(j, _):
                arrival(kv.at[a, j], kv_recv.at[a, j]).wait_recv()
                first_pass(j, False)
                return 0

            first_pass(local, True)
            lax.fori_loop(0, local, first_step, 0)

            def second_step(j, _):
                dprob = dot_nt(kv[a, j, 1], cotangents)
                expo = jnp.exp2((sbuf[j] - rowmax[...]) * to_exp2)
                sbuf[j] = expo
                dbuf[j] = dprob
                rowsum[...] += jnp.sum(expo, axis=0, keepdims=True)
                delta[...] += jnp.sum(expo * dprob, axis=0, keepdims=True)
                return 0

            lax.fori_loop(0, local + 1, second_step, 0)
            rowsum[...] = 1.0 / rowsum[...]
            delta[...] = delta[...] * rowsum[...]

            def third_pass(j):
                prob = sbuf[j] * rowsum[...]
                prob_low = prob.astype(jnp.bfloat16)
                dscore = (prob * (dbuf[j] - delta[...])).astype(jnp.bfloat16)
                oacc[...] += dot_nn(kv[a, j, 1].T, prob_low)
                qacc[...] += dot_nn(kv[a, j, 0].T, dscore)
                return dot_nn(dscore, queries), dot_nn(prob_low, cotangents)

            def third_step(j, _):
                key_part, value_part = third_pass(j)
                gsend[a, j, 0] = key_part.astype(jnp.bfloat16)
                gsend[a, j, 1] = value_part.astype(jnp.bfloat16)
                g_copy(a, j).start()
                return 0

            lax.fori_loop(0, local, third_step, 0)
            gown[a, 0], gown[a, 1] = third_pass(local)
            for h in range(group):
                cols = slice((a * group + h) * HD, (a * group + h + 1) * HD)
                part = slice(h * tok, (h + 1) * tok)
                ostage[:, cols] = oacc[:, part].T.astype(jnp.bfloat16)
                qstage[:, cols] = (scale * qacc[:, part]).T.astype(jnp.bfloat16)

    if loop_refs:
        any_count(*loop_refs)
    else:
        for count in range(1, reach + 1):
            pl.when(local + 1 == count)(functools.partial(one_count, count))

    stores = [
        pltpu.make_async_copy(ostage, att_hbm, store_sem.at[0]),
        pltpu.make_async_copy(qstage, gq_hbm, store_sem.at[1]),
    ]
    for copy in stores:
        copy.start()

    for a in range(heads):

        def collect(j, _, a=a):
            arrival(grecv.at[a, j], g_recv.at[a, j]).wait_recv()
            gown[a] += grecv[a, j].astype(jnp.float32)
            return 0

        lax.fori_loop(local + 1, after, collect, 0)
        cols = slice(a * HD, (a + 1) * HD)
        gk_ref[:, cols] = (scale * gown[a, 0]).astype(jnp.bfloat16)
        gv_ref[:, cols] = gown[a, 1].astype(jnp.bfloat16)

    for copy in stores:
        copy.wait()

    def end_l(target, _):
        @pl.when(target != idx)
        def _():
            l_copy(target).wait_send()

        return 0

    lax.fori_loop(reach, devices, end_l, 0)
    for a in range(heads):

        def end_kv(target, _, a=a):
            kv_copy(a, target).wait_send()
            return 0

        def end_g(j, _, a=a):
            g_copy(a, j).wait_send()
            return 0

        lax.fori_loop(local + 1, after, end_kv, 0)
        lax.fori_loop(0, local, end_g, 0)


def hand_on(pieces, *refs):
    sources, targets, buffers = refs[0:4], refs[4:8], refs[8:12]
    in_sem, out_sem = refs[12:]
    copies = []
    for n in range(4):
        size = sources[n].shape[0] // pieces[n]
        for m in range(pieces[n]):
            part = pl.ds(m * size, size)
            copies.append(
                (
                    pltpu.make_async_copy(
                        sources[n].at[part], buffers[n].at[part], in_sem.at[n, m]
                    ),
                    pltpu.make_async_copy(
                        buffers[n].at[part], targets[n].at[part], out_sem.at[n, m]
                    ),
                )
            )
    for first, _ in copies:
        first.start()
    for first, second in copies:
        first.wait()
        second.start()
    for _, second in copies:
        second.wait()


def shards(query_rows, key_rows, value_rows, grad_out, lengths):
    tok, width = query_rows.shape
    heads = key_rows.shape[1] // HD
    group = width // HD // heads
    devices = lax.axis_size("seq")
    reach = devices // 2 + 1
    rows = group * tok
    docs = -(-lengths.shape[0] // 8) * 8
    wide = 4 if group % 4 == 0 else 1
    unrolled = reach <= UNROLLED
    held = reach * tok if unrolled else 16
    anywhere = pl.BlockSpec(memory_space=pl.ANY)
    vmem = pl.BlockSpec(memory_space=pltpu.VMEM)
    dma = pltpu.SemaphoreType.DMA
    bf16, f32 = jnp.bfloat16, jnp.float32
    loop_scratch = [
        pltpu.VMEM((reach, tok, rows), f32),
        pltpu.VMEM((reach, tok, rows), f32),
        pltpu.VMEM((HD, rows), f32),
        pltpu.VMEM((HD, rows), f32),
        pltpu.VMEM((1, rows), f32),
        pltpu.VMEM((1, rows), f32),
        pltpu.VMEM((1, rows), f32),
    ]
    pairs = reach * rows * tok * heads
    shapes = (
        jax.ShapeDtypeStruct(query_rows.shape, bf16),
        jax.ShapeDtypeStruct(query_rows.shape, bf16),
        jax.ShapeDtypeStruct(key_rows.shape, bf16),
        jax.ShapeDtypeStruct(value_rows.shape, bf16),
    )
    pieces = (4, 4, 1, 1) if tok % 64 == 0 else (1, 1, 1, 1)
    results = pl.pallas_call(
        functools.partial(kernel, devices),
        out_shape=shapes,
        in_specs=[anywhere] * 4 + [pl.BlockSpec(memory_space=pltpu.SMEM)],
        out_specs=(anywhere, anywhere, vmem, vmem),
        scratch_shapes=[
            pltpu.VMEM((tok, width), bf16),
            pltpu.VMEM((tok, width), bf16),
            pltpu.VMEM((heads, reach, 2, tok, HD), bf16),
            pltpu.VMEM((held, rows), bf16),
            pltpu.VMEM((held, rows), bf16),
            pltpu.VMEM((tok, width), bf16),
            pltpu.VMEM((tok, width), bf16),
            pltpu.VMEM((heads, reach, 2, tok, HD), bf16),
            pltpu.VMEM((heads, reach, 2, tok, HD), bf16),
            pltpu.VMEM((heads, 2, tok, HD), f32),
            pltpu.VMEM((devices, docs, HD), jnp.int32),
            pltpu.VMEM((1, wide * tok), jnp.int32),
            dma((heads, 2)),
            dma((heads, 2)),
            dma((2,)),
            dma((heads, reach)),
            dma((heads, reach)),
            dma((heads, reach)),
            dma((heads, reach)),
            dma((devices,)),
            dma((devices,)),
        ]
        + ([] if unrolled else loop_scratch),
        compiler_params=pltpu.CompilerParams(
            collective_id=0, has_side_effects=True, vmem_limit_bytes=56 * 1024 * 1024
        ),
        cost_estimate=pl.CostEstimate(
            flops=12 * pairs * HD, bytes_accessed=8 * tok * width, transcendentals=pairs
        ),
    )(query_rows, key_rows, value_rows, grad_out, lengths)
    return pl.pallas_call(
        functools.partial(hand_on, pieces),
        out_shape=shapes,
        in_specs=[anywhere] * 4,
        out_specs=(anywhere,) * 4,
        scratch_shapes=[pltpu.VMEM(shape.shape, bf16) for shape in shapes]
        + [dma((4, 4)), dma((4, 4))],
        cost_estimate=pl.CostEstimate(
            flops=0, bytes_accessed=8 * tok * width, transcendentals=0
        ),
    )(*results)


def solution(mesh):
    split = P(("groups", "seq"), "head")
    return jax.shard_map(
        shards,
        mesh=mesh,
        in_specs=(split, split, split, split, P(("groups", "seq"))),
        out_specs=(split, split, split, split),
        check_vma=False,
    )
```
